512 devices in a mesh: gx: 16 (over z, core), gy: 32 (over x, y).
Axes of the slice: x: 4, y: 8, z: 8, core: 2. Of those that a mesh axis runs over, the one named last changes fastest.
Arguments:
- features: bfloat16 [524288, 768], P(('gx', 'gy')), may hold values from -12 to 12
- hidden_weight: bfloat16 [768, 1024], replicated, may hold values from -0.21875 to 0.21875
- class_weight: bfloat16 [1024, 153], replicated, may hold values from -0.1875 to 0.1875
- req_owner: int32 [512, 3072, 1], P(('gx', 'gy')), may hold values from 0 to 511; in each aligned block of 3072 rows (0 to 3071, 3072 to 6143, ..., all dimensions but the last counted through in order) at most 12 rows name the same one
- req_block: int32 [512, 3072], P(('gx', 'gy')), may hold values from 0 to 7
- req_offset: int32 [512, 3072], P(('gx', 'gy')), may hold values from 0 to 127
- hop1_counts: int32 [512, 256], P(('gx', 'gy')), may hold values from 1 to 6, 512 in all within a row
- hop2_counts: int32 [512, 768], P(('gx', 'gy')), may hold values from 1 to 8, 2304 in all within a row
- prior_agg: bfloat16 [393216, 768], P(('gx', 'gy')), may hold values from -6 to 6
- prior_hop1: int32 [512, 256], P(('gx', 'gy')), may hold values from 1 to 6, 512 in all within a row
- cotangent: bfloat16 [131072, 153], P(('gx', 'gy')), may hold values from -0.119628906 to 0.119628906
Outputs:
- logits: float32 [131072, 153], P(('gx', 'gy'))
- hidden_grad: float32 [768, 1024], P(None, ('gx', 'gy'))
- class_grad: float32 [1024, 153], replicated
The draws below stay inside these ranges and needn't reach their ends.
Inputs may be any that keep to these rules, and one draw needn't show every extreme that they name: `req_owner`: among the 3072 reads of one device, no owner is named more than 12 times, a bound that some block reaches. `hop1_counts`: each device's row sums to 512. `hop2_counts`: each device's row sums to 2304. `prior_hop1`: each device's row sums to 512.
All inputs are finite; a program needn't handle non-finite values.
Results may differ from the reference program's by a relative error of at most 0.0048.
Values may be sent and summed in bfloat16 or wider, within the bound.
No kernel may reach another device: no remote copies, remote signals or barrier semaphores. Data moves between devices by JAX's collectives and lax.ppermute only.
A program may use at most 128 MiB of HBM per device.

```python
import math
import jax
import jax.numpy as jnp
import numpy as np
from jax import lax

FEAT = 768
HID = 1024
CLASSES = 153
SEEDS = 256
BLK_DEV = 8
BLOCK_ROWS = 128
MOST1 = 6
MOST2 = 8
NODES1 = 768
REQ_DEV = 3072
CAP = 12
ROWS_DEV = 1024
NODES = 524288
TOTAL_SEEDS = 131072
TOTAL_NODES1 = 393216
DEVICES = 512


def with_ends(drawn, stream_key, low, high):
    spot = [jax.random.randint(jax.random.fold_in(stream_key, axis), (), 0, length) for axis, length in enumerate(drawn.shape)]
    longest = drawn.shape.index(max(drawn.shape))
    next_to = spot[:longest] + [(spot[longest] + 1) % drawn.shape[longest]] + spot[longest + 1:]
    return drawn.at[tuple(spot)].set(low).at[tuple(next_to)].set(high)


def steps_of(rng, dims, split, smallest, top_value):
    def one(axis_at, parts):
        steps = jax.random.uniform(jax.random.fold_in(jax.random.fold_in(rng, 6), axis_at), (parts,), jnp.float32, smallest / len(split), top_value / len(split))
        return jnp.repeat(jnp.exp(steps), dims[axis_at] // parts).reshape((-1,) + (1,) * (len(dims) - axis_at - 1))

    gain = one(*split[0])
    for cut in split[1:]:
        gain = gain * one(*cut)
    return gain


def split_up(amount, total, bound, skew):
    portions = [(1 << 20) // math.isqrt(rank ** skew) + 1 for rank in range(2, amount + 1)]
    spare, holding = total - bound - (amount - 1), [1] * (amount - 1)
    while spare > 0:
        movable = [i for i in range(amount - 1) if holding[i] < bound]
        pool, remaining = sum([portions[i] for i in movable]), spare
        for i in movable:
            extra = min(bound - holding[i], max(1, remaining * portions[i] // pool), spare)
            holding[i] = holding[i] + extra
            spare = spare - extra
    return np.array([bound] + holding)


def uneven_parts(own_key, count, total, reach, slope):
    if count == 2:
        one = jax.random.randint(own_key, (), max(1, total - reach), min(reach, total - 1) + 1)
        return jnp.stack([one, total - one])
    sizes = jnp.asarray(split_up(count, total, reach, slope), jnp.int32)
    twos = (count - 1) // 2
    source_of, sink = sizes[1:1 + 2 * twos:2], sizes[2:2 + 2 * twos:2]
    slack = jnp.minimum(source_of - 1, reach - sink)
    shifted = jax.random.randint(jax.random.fold_in(own_key, 1), (twos,), 0, 1 << 20) % (slack + 1)
    sizes = sizes.at[1:1 + 2 * twos:2].set(source_of - shifted).at[2:2 + 2 * twos:2].set(sink + shifted)
    return sizes[jax.random.permutation(jax.random.fold_in(own_key, 2), count)]


def assign_block(key, own, number, rows, amount, top, reach, skew):
    sequence = jax.random.permutation(key, amount)
    packed, usual = shares(amount, rows * top, reach, skew, True), shares(amount, rows * top, reach, skew, False)
    places = jnp.arange(amount)

    def named(sizes, turn):
        used = int((sizes > 0).sum())
        fixed = max(1, used // 4)
        shifted = fixed + (places - fixed + turn * (used - fixed)) % max(1, amount - fixed)
        return jnp.zeros((amount,), jnp.int32).at[sequence[jnp.where(places < fixed, places, shifted)]].set(jnp.asarray(sizes, jnp.int32))

    sizes = jnp.where(number % 4 == 0, named(packed, number // 4), named(usual, number - number // 4 - 1))
    mixed = jax.random.permutation(jax.random.fold_in(own, 3), amount)
    source_of, receiver = mixed[0:amount // 2 * 2:2], mixed[1:amount // 2 * 2:2]
    room = jnp.minimum(sizes[source_of] - 1, reach - sizes[receiver]) // 2
    room = jnp.where((source_of == sequence[0]) | (receiver == sequence[0]) | (sizes[receiver] == 0), 0, jnp.maximum(room, 0))
    shifted = jax.random.randint(jax.random.fold_in(own, 4), (amount // 2,), 0, 1 << 20) % (room + 1)
    sizes = sizes.at[source_of].add(-shifted).at[receiver].add(shifted)
    items = jnp.searchsorted(jnp.cumsum(sizes), jnp.arange(rows * top), side="right").astype(jnp.int32)
    listing = items.reshape(top, rows).T
    listing = listing[jax.random.permutation(jax.random.fold_in(own, 1), rows)]
    turn = jax.random.randint(jax.random.fold_in(own, 2), (rows, 1), 0, top)
    return jnp.take_along_axis(listing, (jnp.arange(top)[None, :] + turn) % top, axis=1)


def shares(amount, total, limit, skew, full):
    loads = [(1 << 20) // math.isqrt(grade ** skew) + 1 for grade in range(1, amount + 1)]
    largest = limit if full else min(limit, max(-(-total // amount), total * loads[0] // sum(loads)))
    least = 1 if total - largest >= amount - 1 else 0
    holding, rest = [largest] + [least] * (amount - 1), total - largest - least * (amount - 1)
    while rest > 0:
        movable = [i for i in range(1, amount) if holding[i] < largest] or [i for i in range(1, amount) if holding[i] < limit]
        pool, remaining = sum([loads[i] for i in movable]), rest
        for i in movable:
            addition = min(limit - holding[i], max(1, remaining * loads[i] // pool), rest)
            holding[i] = holding[i] + addition
            rest = rest - addition
    return np.array(holding)


def centred(rng, extent, scale, most, split=(), kind=jnp.bfloat16):
    loudness = steps_of(rng, extent, split, -0.22, 0.18) if split else 1.0
    array = jax.random.normal(rng, extent, jnp.float32) * scale * loudness
    return jnp.minimum(jnp.maximum(array, -most), most).astype(kind)


def setup_inputs(seed: int = 0) -> dict:
    key_list = jax.random.split(jax.random.key(seed), 12)
    features = centred(key_list[0], (NODES, FEAT), 2.0, 12.0, ((0, 512),))
    hidden_weight = centred(key_list[1], (FEAT, HID), FEAT ** -0.5, 0.21875)
    class_weight = centred(key_list[2], (HID, CLASSES), HID ** -0.5, 0.1875)
    req_owner_keys = jax.random.split(jax.random.fold_in(key_list[3], 1), DEVICES * REQ_DEV // REQ_DEV)
    req_owner_turns = jax.random.permutation(jax.random.fold_in(key_list[3], 3), DEVICES * REQ_DEV // REQ_DEV)
    req_owner = jax.vmap(lambda own, number: assign_block(jax.random.fold_in(key_list[3], 2), own, number, REQ_DEV, DEVICES, 1, CAP, 2))(req_owner_keys, req_owner_turns).reshape((DEVICES, REQ_DEV, 1))
    req_block = with_ends(jax.random.randint(key_list[4], (DEVICES, REQ_DEV), 0, BLK_DEV), jax.random.fold_in(key_list[4], 1), 0, BLK_DEV - 1).astype(jnp.int32)
    req_offset = with_ends(jax.random.randint(key_list[5], (DEVICES, REQ_DEV), 0, BLOCK_ROWS), jax.random.fold_in(key_list[5], 1), 0, BLOCK_ROWS - 1).astype(jnp.int32)
    hop1_counts = jax.vmap(lambda own: uneven_parts(own, SEEDS, 2 * SEEDS, MOST1, 2))(jax.random.split(key_list[6], DEVICES)).reshape((DEVICES, SEEDS)).astype(jnp.int32)
    hop2_counts = jax.vmap(lambda own: uneven_parts(own, NODES1, 3 * NODES1, MOST2, 2))(jax.random.split(key_list[7], DEVICES)).reshape((DEVICES, NODES1)).astype(jnp.int32)
    prior_agg = centred(key_list[8], (TOTAL_NODES1, FEAT), 1.0, 6.0, ((0, 512),))
    prior_hop1 = jax.vmap(lambda own: uneven_parts(own, SEEDS, 2 * SEEDS, MOST1, 2))(jax.random.split(key_list[9], DEVICES)).reshape((DEVICES, SEEDS)).astype(jnp.int32)
    cotangent = centred(key_list[10], (TOTAL_SEEDS, CLASSES), 0.02, 0.119628906, ((0, 512),))
    return {"features": features, "hidden_weight": hidden_weight, "class_weight": class_weight, "req_owner": req_owner, "req_block": req_block, "req_offset": req_offset, "hop1_counts": hop1_counts, "hop2_counts": hop2_counts, "prior_agg": prior_agg, "prior_hop1": prior_hop1, "cotangent": cotangent}


def segment_ids(counts, total):
    ends = jnp.cumsum(counts).astype(jnp.int32)
    positions = jnp.arange(total, dtype=jnp.int32)
    return jnp.searchsorted(ends, positions, side="right").astype(jnp.int32)


def second_layer(agg_one, hop1_counts, hidden_weight):
    nodes = agg_one.shape[0]
    seeds = hop1_counts.shape[0]
    pre_act = jnp.dot(agg_one, hidden_weight, preferred_element_type=jnp.float32)
    sigma = jax.nn.sigmoid(pre_act)
    hidden = (pre_act * sigma).astype(jnp.bfloat16)
    hop1_ids = segment_ids(hop1_counts, nodes - seeds)
    scale_two = 1.0 / (1.0 + hop1_counts.astype(jnp.float32))
    summed_two = jax.ops.segment_sum(hidden[seeds:].astype(jnp.float32), hop1_ids, num_segments=seeds)
    agg_two = ((hidden[:seeds].astype(jnp.float32) + summed_two) * scale_two[:, None]).astype(jnp.bfloat16)
    return pre_act, sigma, hop1_ids, scale_two, agg_two


def forward_pass(fetched, hop1_counts, hop2_counts, hidden_weight, class_weight):
    nodes = hop2_counts.shape[0]
    hop2_ids = segment_ids(hop2_counts, fetched.shape[0] - nodes)
    summed = jax.ops.segment_sum(fetched[nodes:].astype(jnp.float32), hop2_ids, num_segments=nodes)
    agg_one = ((fetched[:nodes].astype(jnp.float32) + summed) / (1.0 + hop2_counts.astype(jnp.float32))[:, None]).astype(jnp.bfloat16)
    agg_two = second_layer(agg_one, hop1_counts, hidden_weight)[4]
    return jnp.dot(agg_two, class_weight, preferred_element_type=jnp.float32)


def backward_pass(prior_agg, prior_hop1, cotangent, hidden_weight, class_weight):
    pre_act, sigma, hop1_ids, scale_two, agg_two = second_layer(prior_agg, prior_hop1, hidden_weight)
    class_term = jnp.dot(agg_two.T, cotangent, preferred_element_type=jnp.float32)
    d_agg = jnp.dot(cotangent, class_weight.T, preferred_element_type=jnp.float32) * scale_two[:, None]
    d_hidden = jnp.concatenate([d_agg, d_agg[hop1_ids]], axis=0)
    d_pre = (d_hidden * sigma * (1.0 + pre_act * (1.0 - sigma))).astype(jnp.bfloat16)
    hidden_term = jnp.dot(prior_agg.T, d_pre, preferred_element_type=jnp.float32)
    return class_term, hidden_term


def reference(features, hidden_weight, class_weight, req_owner, req_block, req_offset, hop1_counts, hop2_counts, prior_agg, prior_hop1, cotangent):
    cot_dev = cotangent.reshape(DEVICES, SEEDS, CLASSES)
    agg_dev = prior_agg.reshape(DEVICES, NODES1, FEAT)

    def one_device(carry, inputs):
        owners, blocks, offsets, counts_one, counts_two, prior_rows, prior_counts, cot_rows = inputs
        rows = (owners.reshape(-1) * ROWS_DEV + blocks * BLOCK_ROWS + offsets).astype(jnp.int32)
        fetched = features[rows]
        logits = forward_pass(fetched, counts_one, counts_two, hidden_weight, class_weight)
        class_term, hidden_term = backward_pass(prior_rows, prior_counts, cot_rows, hidden_weight, class_weight)
        return (carry[0] + hidden_term, carry[1] + class_term), logits

    start = (jnp.zeros((FEAT, HID), jnp.float32), jnp.zeros((HID, CLASSES), jnp.float32))
    totals, logits = lax.scan(one_device, start, (req_owner, req_block, req_offset, hop1_counts, hop2_counts, agg_dev, prior_hop1, cot_dev))
    return logits.reshape(DEVICES * SEEDS, CLASSES), totals[0], totals[1]
```

```python
import jax
import jax.numpy as jnp
from jax import lax
from jax.experimental import pallas as pl
from jax.experimental.pallas import tpu as pltpu
from jax.sharding import PartitionSpec as P

BLOCK_ROWS = 128
DEVICES = 512
CAP = 12
LANES_CAP = 16
FIRST = 8
BOTH = ("gx", "gy")
F32 = jnp.float32
BF16 = jnp.bfloat16
MIB = 1 << 20


def iota(shape, dim):
    return lax.broadcasted_iota(jnp.int32, shape, dim)


def dot(a, b, dims=((1,), (0,))):
    return lax.dot_general(a, b, (dims, ((), ())), preferred_element_type=F32)


def params(mib, semantics=("arbitrary",)):
    return pltpu.CompilerParams(dimension_semantics=semantics, vmem_limit_bytes=mib * MIB)


def route_kernel(owner_ref, block_ref, offset_ref, hop2_ref, want_ref, node_ref):
    nodes = hop2_ref.shape[1]
    step = 256
    counts = hop2_ref[...].astype(F32)
    ends = jnp.sum(
        jnp.where(iota((nodes, nodes), 1) <= iota((nodes, nodes), 0), counts, 0.0),
        axis=1,
        keepdims=True,
    )
    before = (iota((step, step), 0) < iota((step, step), 1)).astype(BF16)
    owner_at = iota((DEVICES, step), 0)
    slot_at = iota((LANES_CAP, step), 0)
    carry = jnp.zeros((DEVICES, 1), F32)
    total = jnp.zeros((DEVICES, 2 * LANES_CAP), F32)
    for blk in range(owner_ref.shape[1] // step):
        at = pl.ds(blk * step, step)
        place = blk * step + iota((1, step), 1)
        if blk * step < nodes:
            node = place
        else:
            inside = (place - nodes).astype(F32)
            node = jnp.sum(jnp.where(ends <= inside, 1.0, 0.0), axis=0, keepdims=True).astype(
                jnp.int32
            )
        want = block_ref[:, at] * BLOCK_ROWS + offset_ref[:, at]
        here = owner_at == owner_ref[:, at]
        here_f = jnp.where(here, 1.0, 0.0)
        here_b = here_f.astype(BF16)
        seen = dot(here_b, before) + carry
        rank = jnp.sum(jnp.where(here, seen, 0.0), axis=0, keepdims=True).astype(jnp.int32)
        carry = carry + jnp.sum(here_f, axis=1, keepdims=True)
        mine = slot_at == rank

        def fields(part):
            return jnp.concatenate(
                [
                    jnp.where(mine, part(want + 1).astype(F32), 0.0),
                    jnp.where(mine, part(node + 1).astype(F32), 0.0),
                ],
                axis=0,
            ).astype(BF16)

        total = total + dot(here_b, fields(lambda v: v & ~31), ((1,), (1,)))
        total = total + dot(here_b, fields(lambda v: v & 31), ((1,), (1,)))
    total = total.astype(jnp.int32)
    want_ref[...] = total[:, :LANES_CAP]
    node_ref[...] = total[:, LANES_CAP:]


def route(owners, blocks, offsets, hop2):
    shape = jax.ShapeDtypeStruct((DEVICES, LANES_CAP), jnp.int32)
    return pl.pallas_call(
        route_kernel,
        out_shape=(shape, shape),
        compiler_params=pltpu.CompilerParams(vmem_limit_bytes=32 * MIB),
        cost_estimate=pl.CostEstimate(flops=4_000_000_000, bytes_accessed=200_000, transcendentals=0),
        name="route",
    )(owners, blocks, offsets, hop2)


def gather_kernel(folded, want_ref, features_ref, out_ref):
    readers, lanes = want_ref.shape
    rows = readers * 8
    spread = jnp.broadcast_to(want_ref[...].astype(F32)[:, None, :], (readers, 8, lanes))
    sub = iota((readers, 8, lanes), 1)
    slot = FIRST + (sub & 3) if folded else sub
    chosen = jnp.sum(
        jnp.where(iota((readers, 8, lanes), 2) == slot, spread, 0.0), axis=2, keepdims=True
    )
    chosen = chosen.reshape(rows, 1).astype(jnp.int32) - 1
    held = features_ref.shape[0]
    picks = jnp.where(iota((rows, held), 1) == chosen, 1.0, 0.0).astype(BF16)
    found = dot(picks, features_ref[...])
    if folded:
        half = found.shape[1] // 2
        low = (iota((rows, half), 0) & 7) < 4
        found = jnp.where(low, found[:, :half], found[:, half:])
    out_ref[...] = found.astype(BF16)


def gather(folded, want, features):
    width = features.shape[1] // 2 if folded else features.shape[1]
    readers = 64
    return pl.pallas_call(
        lambda *refs: gather_kernel(folded, *refs),
        grid=(DEVICES // readers,),
        in_specs=[
            pl.BlockSpec((readers, LANES_CAP), lambda i: (i, 0)),
            pl.BlockSpec(features.shape, lambda i: (0, 0)),
        ],
        out_specs=pl.BlockSpec((readers * 8, width), lambda i: (i, 0)),
        out_shape=jax.ShapeDtypeStruct((DEVICES * 8, width), BF16),
        compiler_params=params(48),
        cost_estimate=pl.CostEstimate(
            flops=2 * DEVICES * 8 * features.shape[0] * features.shape[1],
            bytes_accessed=DEVICES * 16 * width,
            transcendentals=0,
        ),
        name="gather_rest" if folded else "gather_first",
    )(want, features)


def sum_first_kernel(node_ref, rows_ref, out_ref):
    nodes, step = out_ref.shape[0], rows_ref.shape[0]
    takes = jnp.where(iota((nodes, step), 0) == node_ref[...] - 1, 1.0, 0.0).astype(BF16)
    part = dot(takes, rows_ref[...])

    @pl.when(pl.program_id(0) == 0)
    def _():
        out_ref[...] = part

    @pl.when(pl.program_id(0) > 0)
    def _():
        out_ref[...] += part


def sum_first(node, rows, nodes):
    step = 512
    count, width = rows.shape
    return pl.pallas_call(
        sum_first_kernel,
        grid=(count // step,),
        in_specs=[
            pl.BlockSpec((1, step), lambda i: (0, i)),
            pl.BlockSpec((step, width), lambda i: (i, 0)),
        ],
        out_specs=pl.BlockSpec((nodes, width), lambda i: (0, 0)),
        out_shape=jax.ShapeDtypeStruct((nodes, width), F32),
        compiler_params=params(48),
        cost_estimate=pl.CostEstimate(
            flops=2 * nodes * count * width, bytes_accessed=count * width * 2, transcendentals=0
        ),
        name="sum_first",
    )(node, rows)


def seed_groups(counts, nodes):
    seeds = counts.shape[1]
    row, col = iota((seeds, seeds), 0), iota((seeds, seeds), 1)
    ends = jnp.sum(jnp.where(col <= row, counts, 0.0), axis=1, keepdims=True)
    own = jnp.sum(jnp.where(col == row, counts, 0.0), axis=1, keepdims=True)
    seed, node = iota((seeds, nodes), 0), iota((seeds, nodes), 1)
    inside = (node - seeds).astype(F32)
    grouped = (node >= seeds) & (inside >= ends - own) & (inside < ends)
    return jnp.where(grouped | (seed == node), 1.0, 0.0).astype(BF16), 1.0 + own


def forward_kernel(node_ref, rows_ref, sums_ref, hop1_ref, hop2_ref, w1_ref, w2_ref, out_ref, acc_ref):
    nodes, step = sums_ref.shape[0], rows_ref.shape[0]
    half = rows_ref.shape[1]

    @pl.when(pl.program_id(0) == 0)
    def _():
        acc_ref[...] = sums_ref[...]

    takes = iota((nodes, step), 0) == node_ref[...] - 1
    low = (iota((nodes, step), 1) & 7) < 4
    acc_ref[:, :half] += dot(jnp.where(takes & low, 1.0, 0.0).astype(BF16), rows_ref[...])
    acc_ref[:, half:] += dot(
        jnp.where(takes & jnp.logical_not(low), 1.0, 0.0).astype(BF16), rows_ref[...]
    )

    @pl.when(pl.program_id(0) == pl.num_programs(0) - 1)
    def _():
        same = iota((nodes, nodes), 0) == iota((nodes, nodes), 1)
        counts = jnp.sum(
            jnp.where(same, hop2_ref[...].astype(F32), 0.0), axis=1, keepdims=True
        )
        agg_one = (acc_ref[...] / (1.0 + counts)).astype(BF16)
        groups, sizes = seed_groups(hop1_ref[...].astype(F32), nodes)
        scale = 1.0 / sizes
        total = jnp.zeros(out_ref.shape, F32)
        hid = w1_ref.shape[1]
        for at in range(0, hid, 256):
            pre = dot(agg_one, w1_ref[:, at : at + 256])
            hidden = (pre * jax.nn.sigmoid(pre)).astype(BF16)
            agg_two = (dot(groups, hidden) * scale).astype(BF16)
            total = total + dot(agg_two, w2_ref[at : at + 256, :])
        out_ref[...] = total


def forward(node, rows, sums, hop1, hop2, w1, w2):
    step = 512
    count, half = rows.shape
    nodes, width = sums.shape
    seeds, classes = hop1.shape[1], w2.shape[1]
    whole = lambda a: pl.BlockSpec(a.shape, lambda i: (0, 0))
    return pl.pallas_call(
        forward_kernel,
        grid=(count // step,),
        in_specs=[
            pl.BlockSpec((1, step), lambda i: (0, i)),
            pl.BlockSpec((step, half), lambda i: (i, 0)),
            whole(sums),
            whole(hop1),
            whole(hop2),
            whole(w1),
            whole(w2),
        ],
        out_specs=pl.BlockSpec((seeds, classes), lambda i: (0, 0)),
        out_shape=jax.ShapeDtypeStruct((seeds, classes), F32),
        scratch_shapes=[pltpu.VMEM((nodes, width), F32)],
        compiler_params=params(56),
        cost_estimate=pl.CostEstimate(
            flops=2 * nodes * count * width + 2 * nodes * width * w1.shape[1],
            bytes_accessed=count * half * 2,
            transcendentals=nodes * w1.shape[1],
        ),
        name="forward",
    )(node, rows, sums, hop1, hop2, w1, w2)


def backward_kernel(agg_ref, hop1_ref, cot_ref, w1_ref, w2_ref, hidden_ref, class_ref):
    nodes = agg_ref.shape[0]
    seeds = hop1_ref.shape[1]
    counts = hop1_ref[...].astype(F32)
    groups, sizes = seed_groups(counts, nodes)
    scale = 1.0 / sizes
    row, col = iota((seeds, seeds), 0), iota((seeds, seeds), 1)
    own = sizes - 1.0
    ends = jnp.sum(jnp.where(row <= col, own, 0.0), axis=0, keepdims=True)
    node, seed = iota((nodes, seeds), 0), iota((nodes, seeds), 1)
    inside = (node - seeds).astype(F32)
    grouped = (node >= seeds) & (inside >= ends - counts) & (inside < ends)
    hands = grouped | (seed == node)
    node_scale = jnp.sum(jnp.where(hands, 1.0 / (1.0 + counts), 0.0), axis=1, keepdims=True)
    cot = cot_ref[...]
    node_cot = dot(jnp.where(hands, 1.0, 0.0).astype(BF16), cot).astype(BF16)

    agg = agg_ref[...]
    pre = dot(agg, w1_ref[...])
    sigma = jax.nn.sigmoid(pre)
    hidden = (pre * sigma).astype(BF16)
    agg_two = (dot(groups, hidden) * scale).astype(BF16)
    class_ref[...] = dot(agg_two, cot, ((0,), (0,)))
    d_hidden = dot(node_cot, w2_ref[...], ((1,), (1,))) * node_scale
    d_pre = (d_hidden * sigma * (1.0 + pre * (1.0 - sigma))).astype(BF16)
    hidden_ref[...] = dot(d_pre, agg, ((0,), (0,)))


def backward(agg, hop1, cot, w1, w2):
    nodes, feat = agg.shape
    hid = w1.shape[1]
    seeds, classes = cot.shape
    step = 256
    whole = lambda a: pl.BlockSpec(a.shape, lambda i: (0, 0))
    return pl.pallas_call(
        backward_kernel,
        grid=(hid // step,),
        in_specs=[
            whole(agg),
            whole(hop1),
            whole(cot),
            pl.BlockSpec((feat, step), lambda i: (0, i)),
            pl.BlockSpec((step, classes), lambda i: (i, 0)),
        ],
        out_specs=(
            pl.BlockSpec((step, feat), lambda i: (i, 0)),
            pl.BlockSpec((step, classes), lambda i: (i, 0)),
        ),
        out_shape=(
            jax.ShapeDtypeStruct((hid, feat), F32),
            jax.ShapeDtypeStruct((hid, classes), F32),
        ),
        compiler_params=params(56),
        cost_estimate=pl.CostEstimate(
            flops=4 * nodes * feat * hid, bytes_accessed=6 * MIB, transcendentals=nodes * hid
        ),
        name="backward",
    )(agg, hop1, cot, w1, w2)


def exchange(rows):
    return lax.all_to_all(rows, BOTH, split_axis=0, concat_axis=0, tiled=True)


def on_device(
    features,
    hidden_weight,
    class_weight,
    req_owner,
    req_block,
    req_offset,
    hop1_counts,
    hop2_counts,
    prior_agg,
    prior_hop1,
    cotangent,
):
    outer, inner = lax.axis_size("gx"), lax.axis_size("gy")
    want, node = route(req_owner.reshape(1, -1), req_block, req_offset, hop2_counts)
    asked = lax.all_to_all(
        lax.all_to_all(
            want.reshape(outer, inner, LANES_CAP), "gx", split_axis=0, concat_axis=0, tiled=True
        ),
        "gy",
        split_axis=1,
        concat_axis=1,
        tiled=True,
    ).reshape(DEVICES, LANES_CAP)
    first = exchange(gather(False, asked, features))
    rest = exchange(gather(True, asked, features))

    hidden_term, class_term = backward(
        prior_agg, prior_hop1, cotangent, hidden_weight, class_weight
    )
    hidden_grad = lax.psum_scatter(hidden_term, "gx", scatter_dimension=0, tiled=True)
    hidden_grad = lax.psum_scatter(hidden_grad, "gy", scatter_dimension=0, tiled=True).T
    class_grad = lax.psum(class_term, BOTH)

    nodes = hop2_counts.shape[1]
    node_first = node[:, :FIRST].reshape(1, -1)
    tail = node[:, FIRST:CAP]
    node_rest = jnp.concatenate([tail, tail], axis=1).reshape(1, -1)
    sums = sum_first(node_first, first, nodes)
    logits = forward(
        node_rest, rest, sums, hop1_counts, hop2_counts, hidden_weight, class_weight
    )
    return (logits, hidden_grad, class_grad)


def solution(mesh):
    placed = (
        P(BOTH, None),
        P(),
        P(),
        P(BOTH, None, None),
        P(BOTH, None),
        P(BOTH, None),
        P(BOTH, None),
        P(BOTH, None),
        P(BOTH, None),
        P(BOTH, None),
        P(BOTH, None),
    )
    return jax.shard_map(
        on_device,
        mesh=mesh,
        in_specs=placed,
        out_specs=(P(BOTH, None), P(None, BOTH), P()),
        check_vma=False,
    )
```

```python
import jax
import jax.numpy as jnp
from jax import lax
from jax.experimental import pallas as pl
from jax.experimental.pallas import tpu as pltpu
from jax.sharding import PartitionSpec as P

BLOCK_ROWS = 128
DEVICES = 512
CAP = 12
LANES_CAP = 16
FIRST = 8
PIECE = 128
BOTH = ("gx", "gy")
Z, CORES, X, Y = 8, 2, 4, 8
F32 = jnp.float32
BF16 = jnp.bfloat16
MIB = 1 << 20


def iota(shape, dim):
    return lax.broadcasted_iota(jnp.int32, shape, dim)


def dot(a, b, dims=((1,), (0,))):
    return lax.dot_general(a, b, (dims, ((), ())), preferred_element_type=F32)


def params(mib, semantics=("arbitrary",)):
    return pltpu.CompilerParams(dimension_semantics=semantics, vmem_limit_bytes=mib * MIB)


def route_kernel(owner_ref, block_ref, offset_ref, hop2_ref, want_ref, node_ref):
    nodes = hop2_ref.shape[1]
    step = 256
    counts = hop2_ref[...].astype(F32)
    ends = jnp.sum(
        jnp.where(iota((nodes, nodes), 1) <= iota((nodes, nodes), 0), counts, 0.0),
        axis=1,
        keepdims=True,
    )
    before = (iota((step, step), 0) < iota((step, step), 1)).astype(BF16)
    owner_at = iota((DEVICES, step), 0)
    slot_at = iota((LANES_CAP, step), 0)
    carry = jnp.zeros((DEVICES, 1), F32)
    total = jnp.zeros((DEVICES, 2 * LANES_CAP), F32)
    for blk in range(owner_ref.shape[1] // step):
        at = pl.ds(blk * step, step)
        place = blk * step + iota((1, step), 1)
        if blk * step < nodes:
            node = place
        else:
            inside = (place - nodes).astype(F32)
            node = jnp.sum(jnp.where(ends <= inside, 1.0, 0.0), axis=0, keepdims=True).astype(
                jnp.int32
            )
        want = block_ref[:, at] * BLOCK_ROWS + offset_ref[:, at]
        here = owner_at == owner_ref[:, at]
        here_f = jnp.where(here, 1.0, 0.0)
        here_b = here_f.astype(BF16)
        seen = dot(here_b, before) + carry
        rank = jnp.sum(jnp.where(here, seen, 0.0), axis=0, keepdims=True).astype(jnp.int32)
        carry = carry + jnp.sum(here_f, axis=1, keepdims=True)
        mine = slot_at == rank

        def fields(part):
            return jnp.concatenate(
                [
                    jnp.where(mine, part(want + 1).astype(F32), 0.0),
                    jnp.where(mine, part(node + 1).astype(F32), 0.0),
                ],
                axis=0,
            ).astype(BF16)

        total = total + dot(here_b, fields(lambda v: v & ~31), ((1,), (1,)))
        total = total + dot(here_b, fields(lambda v: v & 31), ((1,), (1,)))
    total = total.astype(jnp.int32)
    want_ref[...] = total[:, :LANES_CAP]
    node_ref[...] = total[:, LANES_CAP:]


def route(owners, blocks, offsets, hop2):
    shape = jax.ShapeDtypeStruct((DEVICES, LANES_CAP), jnp.int32)
    return pl.pallas_call(
        route_kernel,
        out_shape=(shape, shape),
        compiler_params=pltpu.CompilerParams(vmem_limit_bytes=32 * MIB),
        cost_estimate=pl.CostEstimate(flops=4_000_000_000, bytes_accessed=200_000, transcendentals=0),
        name="route",
    )(owners, blocks, offsets, hop2)


def picks_of(want_ref, held, slot_of):
    readers, lanes = want_ref.shape
    rows = readers * 8
    spread = jnp.broadcast_to(want_ref[...].astype(F32)[:, None, :], (readers, 8, lanes))
    slot = slot_of(iota((readers, 8, lanes), 1))
    chosen = jnp.sum(
        jnp.where(iota((readers, 8, lanes), 2) == slot, spread, 0.0), axis=2, keepdims=True
    )
    chosen = chosen.reshape(rows, 1).astype(jnp.int32) - 1
    return jnp.where(iota((rows, held), 1) == chosen, 1.0, 0.0).astype(BF16)


def gather_kernel(part, want_ref, features_ref, after_ref, out_ref):
    held = features_ref.shape[0]
    if part == 1:
        found = dot(picks_of(want_ref, held, lambda sub: FIRST + (sub & 3)), features_ref[...])
        half = found.shape[1] // 2
        low = (iota((found.shape[0], half), 0) & 7) < 4
        out_ref[...] = jnp.where(low, found[:, :half], found[:, half:]).astype(BF16)
        return
    half = features_ref.shape[1]
    found = dot(picks_of(want_ref, held, lambda sub: sub), features_ref[...])
    out_ref[:, :half] = found.astype(BF16)
    if part == 2:
        last = dot(
            picks_of(want_ref, held, lambda sub: jnp.where(sub < 2, CAP - 2 + sub, LANES_CAP)),
            features_ref[:, half - PIECE :],
        )
        out_ref[:, half:] = last.astype(BF16)


def gather(part, want, features, after):
    held, width = features.shape
    half = width // 2
    sent = half + PIECE if part == 2 else half
    readers = 64
    if part == 1:
        source = pl.BlockSpec((held, width), lambda i: (0, 0))
    else:
        source = pl.BlockSpec((held, half), lambda i: (0, part // 2))
    return pl.pallas_call(
        lambda *refs: gather_kernel(part, *refs),
        grid=(DEVICES // readers,),
        in_specs=[
            pl.BlockSpec((readers, LANES_CAP), lambda i: (i, 0)),
            source,
            pl.BlockSpec(memory_space=pl.ANY),
        ],
        out_specs=pl.BlockSpec((readers * 8, sent), lambda i: (i, 0)),
        out_shape=jax.ShapeDtypeStruct((DEVICES * 8, sent), BF16),
        compiler_params=params(32),
        cost_estimate=pl.CostEstimate(
            flops=2 * DEVICES * 8 * held * (half if part == 0 else width),
            bytes_accessed=DEVICES * 16 * sent,
            transcendentals=0,
        ),
        name=f"gather_{part}",
    )(want, features, after)


def taken(node_ref, nodes):
    return iota((nodes, node_ref.shape[1]), 0) == node_ref[...] - 1


def zero_one(mask):
    return jnp.where(mask, 1.0, 0.0).astype(BF16)


def add_up(out_ref, part):
    @pl.when(pl.program_id(0) == 0)
    def _():
        out_ref[...] = part

    @pl.when(pl.program_id(0) > 0)
    def _():
        out_ref[...] += part


def whole(a):
    return pl.BlockSpec(a.shape, lambda i: (0,) * a.ndim)


def sum_slots_kernel(node_ref, rows_ref, out_ref):
    add_up(out_ref, dot(zero_one(taken(node_ref, out_ref.shape[0])), rows_ref[...]))


def sum_slots(node, rows, nodes):
    step = 1024
    count, half = rows.shape
    return pl.pallas_call(
        sum_slots_kernel,
        grid=(count // step,),
        in_specs=[
            pl.BlockSpec((1, step), lambda i: (0, i)),
            pl.BlockSpec((step, half), lambda i: (i, 0)),
        ],
        out_specs=pl.BlockSpec((nodes, half), lambda i: (0, 0)),
        out_shape=jax.ShapeDtypeStruct((nodes, half), F32),
        compiler_params=params(32),
        cost_estimate=pl.CostEstimate(
            flops=2 * nodes * count * half, bytes_accessed=count * half * 2, transcendentals=0
        ),
        name="sum_slots",
    )(node, rows)


def group_sizes(hop2_ref):
    nodes = hop2_ref.shape[1]
    same = iota((nodes, nodes), 0) == iota((nodes, nodes), 1)
    counts = jnp.where(same, hop2_ref[...].astype(F32), 0.0)
    return 1.0 + jnp.sum(counts, axis=1, keepdims=True)


def sum_folded_kernel(node_ref, rows_ref, sums_ref, hop2_ref, w1_ref, pre_ref, high_ref, low_ref):
    nodes, half = sums_ref.shape
    takes = taken(node_ref, nodes)
    low = (iota(takes.shape, 1) & 7) < 4
    rows = rows_ref[...]
    ride = rows[:, half - PIECE :].astype(F32)
    ride = jnp.where((iota(ride.shape, 0) & 7) >= 6, 0.0, ride).astype(BF16)
    rows = jnp.concatenate([rows[:, : half - PIECE], ride], axis=1)
    add_up(low_ref, dot(zero_one(takes & low), rows))
    add_up(high_ref, dot(zero_one(takes & jnp.logical_not(low)), rows))

    @pl.when(pl.program_id(0) == pl.num_programs(0) - 1)
    def _():
        agg = ((sums_ref[...] + low_ref[...]) / group_sizes(hop2_ref)).astype(BF16)
        pre_ref[...] = dot(agg, w1_ref[...])


def sum_folded(node, rows, sums, hop2, w1):
    step = 1024
    count, half = rows.shape
    nodes, hid = sums.shape[0], w1.shape[1]
    return pl.pallas_call(
        sum_folded_kernel,
        grid=(count // step,),
        in_specs=[
            pl.BlockSpec((1, step), lambda i: (0, i)),
            pl.BlockSpec((step, half), lambda i: (i, 0)),
            whole(sums),
            whole(hop2),
            pl.BlockSpec((half, hid), lambda i: (0, 0)),
        ],
        out_specs=(
            pl.BlockSpec((nodes, hid), lambda i: (0, 0)),
            pl.BlockSpec((nodes, half), lambda i: (0, 0)),
        ),
        out_shape=(
            jax.ShapeDtypeStruct((nodes, hid), F32),
            jax.ShapeDtypeStruct((nodes, half), F32),
        ),
        scratch_shapes=[pltpu.VMEM((nodes, half), F32)],
        compiler_params=params(48),
        cost_estimate=pl.CostEstimate(
            flops=4 * nodes * count * half, bytes_accessed=count * half * 2, transcendentals=0
        ),
        name="sum_folded",
    )(node, rows, sums, hop2, w1)


def seed_groups(counts, nodes):
    seeds = counts.shape[1]
    row, col = iota((seeds, seeds), 0), iota((seeds, seeds), 1)
    ends = jnp.sum(jnp.where(col <= row, counts, 0.0), axis=1, keepdims=True)
    own = jnp.sum(jnp.where(col == row, counts, 0.0), axis=1, keepdims=True)
    seed, node = iota((seeds, nodes), 0), iota((seeds, nodes), 1)
    inside = (node - seeds).astype(F32)
    grouped = (node >= seeds) & (inside >= ends - own) & (inside < ends)
    return jnp.where(grouped | (seed == node), 1.0, 0.0).astype(BF16), 1.0 + own


def forward_kernel(
    node_ref,
    last_ref,
    rows_ref,
    sums_ref,
    pre_ref,
    hop1_ref,
    hop2_ref,
    w1_ref,
    w2_ref,
    out_ref,
    acc_ref,
):
    nodes, half = sums_ref.shape
    add_up(acc_ref, dot(zero_one(taken(node_ref, nodes)), rows_ref[:, :half]))
    acc_ref[:, half - PIECE :] += dot(zero_one(taken(last_ref, nodes)), rows_ref[:, half:])

    @pl.when(pl.program_id(0) == pl.num_programs(0) - 1)
    def _():
        agg_one = ((sums_ref[...] + acc_ref[...]) / group_sizes(hop2_ref)).astype(BF16)
        groups, sizes = seed_groups(hop1_ref[...].astype(F32), nodes)
        scale = 1.0 / sizes
        total = jnp.zeros(out_ref.shape, F32)
        for at in range(0, w1_ref.shape[1], 256):
            pre = pre_ref[:, at : at + 256] + dot(agg_one, w1_ref[:, at : at + 256])
            hidden = (pre * jax.nn.sigmoid(pre)).astype(BF16)
            agg_two = (dot(groups, hidden) * scale).astype(BF16)
            total = total + dot(agg_two, w2_ref[at : at + 256, :])
        out_ref[...] = total


def forward(node, last, rows, sums, pre, hop1, hop2, w1, w2):
    step = 1024
    count, sent = rows.shape
    nodes, half = sums.shape
    hid = w1.shape[1]
    seeds, classes = hop1.shape[1], w2.shape[1]
    return pl.pallas_call(
        forward_kernel,
        grid=(count // step,),
        in_specs=[
            pl.BlockSpec((1, step), lambda i: (0, i)),
            pl.BlockSpec((1, step), lambda i: (0, i)),
            pl.BlockSpec((step, sent), lambda i: (i, 0)),
            whole(sums),
            whole(pre),
            whole(hop1),
            whole(hop2),
            pl.BlockSpec((half, hid), lambda i: (1, 0)),
            whole(w2),
        ],
        out_specs=pl.BlockSpec((seeds, classes), lambda i: (0, 0)),
        out_shape=jax.ShapeDtypeStruct((seeds, classes), F32),
        scratch_shapes=[pltpu.VMEM((nodes, half), F32)],
        compiler_params=params(48),
        cost_estimate=pl.CostEstimate(
            flops=2 * nodes * count * half + 2 * nodes * half * hid,
            bytes_accessed=count * half * 2,
            transcendentals=nodes * hid,
        ),
        name="forward",
    )(node, last, rows, sums, pre, hop1, hop2, w1, w2)


def backward_kernel(
    core_ref, agg_ref, hop1_ref, cot_ref, w1_ref, w2_ref, after_ref, kept_ref, sent_ref
):
    nodes = agg_ref.shape[0]
    seeds = hop1_ref.shape[1]
    counts = hop1_ref[...].astype(F32)
    groups, sizes = seed_groups(counts, nodes)
    scale = 1.0 / sizes
    row, col = iota((seeds, seeds), 0), iota((seeds, seeds), 1)
    own = sizes - 1.0
    ends = jnp.sum(jnp.where(row <= col, own, 0.0), axis=0, keepdims=True)
    node, seed = iota((nodes, seeds), 0), iota((nodes, seeds), 1)
    inside = (node - seeds).astype(F32)
    grouped = (node >= seeds) & (inside >= ends - counts) & (inside < ends)
    hands = grouped | (seed == node)
    node_scale = jnp.sum(jnp.where(hands, 1.0 / (1.0 + counts), 0.0), axis=1, keepdims=True)
    cot = cot_ref[...]
    node_cot = dot(jnp.where(hands, 1.0, 0.0).astype(BF16), cot).astype(BF16)

    agg = agg_ref[...]
    pre = dot(agg, w1_ref[...])
    sigma = jax.nn.sigmoid(pre)
    hidden = (pre * sigma).astype(BF16)
    agg_two = (dot(groups, hidden) * scale).astype(BF16)
    classes = cot.shape[1]
    wide = zero_one(iota((classes, 2 * PIECE), 0) == iota((classes, 2 * PIECE), 1))
    class_term = dot(agg_two, dot(cot, wide).astype(BF16), ((0,), (0,)))
    d_hidden = dot(node_cot, w2_ref[...], ((1,), (1,))) * node_scale
    d_pre = (d_hidden * sigma * (1.0 + pre * (1.0 - sigma))).astype(BF16)
    hidden_term = dot(d_pre, agg, ((0,), (0,)))
    first = core_ref[0] == 0
    half = kept_ref.shape[1] // 2
    mine = slice(0, half), slice(half, 2 * half)
    low = hidden_term[:, :half], hidden_term[:, half : 2 * half]
    high = hidden_term[:, 2 * half :], class_term
    for at, a, b in zip(mine, low, high):
        kept_ref[:, at] = jnp.where(first, a, b)
        sent_ref[:, at] = jnp.where(first, b, a)


def backward(core, agg, hop1, cot, w1, w2, after):
    nodes, feat = agg.shape
    hid = w1.shape[1]
    classes = cot.shape[1]
    step = 256
    half = (feat + 2 * PIECE) // 2
    return pl.pallas_call(
        backward_kernel,
        grid=(hid // step,),
        in_specs=[
            pl.BlockSpec(memory_space=pltpu.SMEM),
            whole(agg),
            whole(hop1),
            whole(cot),
            pl.BlockSpec((feat, step), lambda i: (0, i)),
            pl.BlockSpec((step, classes), lambda i: (i, 0)),
            pl.BlockSpec(memory_space=pl.ANY),
        ],
        out_specs=[pl.BlockSpec((step, half), lambda i: (i, 0))] * 2,
        out_shape=[jax.ShapeDtypeStruct((hid, half), F32)] * 2,
        compiler_params=params(48),
        cost_estimate=pl.CostEstimate(
            flops=4 * nodes * feat * hid, bytes_accessed=6 * MIB, transcendentals=nodes * hid
        ),
        name="backward",
    )(core, agg, hop1, cot, w1, w2, after)


def swap(rows, axis, bit):
    size = lax.axis_size(axis)
    return lax.ppermute(rows, axis, [(i, i ^ bit) for i in range(size)])


def split_kernel(x_ref, kept_ref, got_ref, own_ref, *sent_refs):
    def piece(k):
        at = pl.ds(pl.multiple_of(k * PIECE, PIECE), PIECE)
        return kept_ref[:, at] + got_ref[:, at]

    x = x_ref[0]
    own_ref[...] = piece(x)
    for k, ref in enumerate(sent_refs, 1):
        ref[...] = piece(x ^ k).astype(BF16)


def split(x, kept, got):
    rows, width = kept.shape
    step = 256
    block = pl.BlockSpec((step, width), lambda i: (i, 0))
    return pl.pallas_call(
        split_kernel,
        grid=(rows // step,),
        in_specs=[pl.BlockSpec(memory_space=pltpu.SMEM), block, block],
        out_specs=[pl.BlockSpec((step, PIECE), lambda i: (i, 0))] * X,
        out_shape=[jax.ShapeDtypeStruct((rows, PIECE), F32)]
        + [jax.ShapeDtypeStruct((rows, PIECE), BF16)] * (X - 1),
        compiler_params=params(16),
        name="split",
    )(x, kept, got)


def ride_sums_kernel(own_ref, *refs):
    got, rows_ref, out_ref = refs[: X - 1], refs[X - 1], refs[X]
    piece = own_ref[...]
    for ref in got:
        piece = piece + ref[...].astype(F32)
    shape = rows_ref.shape[0], piece.shape[0]
    i, j = iota(shape, 0), iota(shape, 1)
    put = dot(zero_one(((i >> 3) == (j >> 1)) & ((i & 7) == 6 + (j & 1))), piece.astype(BF16))
    ride = (iota(rows_ref.shape, 0) & 7) >= 6
    out_ref[...] = jnp.where(ride, put, rows_ref[...].astype(F32)).astype(BF16)


def ride_sums(own, got, rows):
    readers = 64
    mine = pl.BlockSpec((readers * 2, PIECE), lambda i: (i, 0))
    tile = pl.BlockSpec((readers * 8, PIECE), lambda i: (i, rows.shape[1] // PIECE - 1))
    return pl.pallas_call(
        ride_sums_kernel,
        grid=(DEVICES // readers,),
        in_specs=[mine] * X + [tile],
        out_specs=tile,
        out_shape=jax.ShapeDtypeStruct(rows.shape, BF16),
        input_output_aliases={X: 0},
        compiler_params=params(16),
        name="ride_sums",
    )(own, *got, rows)


def own_sums_kernel(rows_ref, out_ref, tile_ref):
    count = rows_ref.shape[0]
    shape = out_ref.shape[0], count
    j, i = iota(shape, 0), pl.program_id(0) * count + iota(shape, 1)
    add_up(out_ref, dot(zero_one((((i >> 6) & 7) == (j >> 1)) & ((i & 7) == 6 + (j & 1))), rows_ref[...]))

    @pl.when(pl.program_id(0) == pl.num_programs(0) - 1)
    def _():
        total = out_ref[...]
        high = total.astype(BF16).astype(F32)
        low = total - high
        tile_ref[...] = jnp.zeros(tile_ref.shape, F32)
        tile_ref[2:4, :] = high[12:14]
        tile_ref[4:6, :] = low[12:14]
        tile_ref[6:7, :] = (
            high[14:15]
            + pltpu.roll(high[15:16], 32, 1)
            + pltpu.roll(low[14:15], 64, 1)
            + pltpu.roll(low[15:16], 96, 1)
        )


def own_sums(rows):
    step = 2048
    return pl.pallas_call(
        own_sums_kernel,
        grid=(rows.shape[0] // step,),
        in_specs=[pl.BlockSpec((step, PIECE), lambda i: (i, rows.shape[1] // PIECE - 1))],
        out_specs=[
            pl.BlockSpec((16, PIECE), lambda i: (0, 0)),
            pl.BlockSpec((8, PIECE), lambda i: (0, 0)),
        ],
        out_shape=[
            jax.ShapeDtypeStruct((16, PIECE), F32),
            jax.ShapeDtypeStruct((8, PIECE), F32),
        ],
        compiler_params=params(16),
        name="own_sums",
    )(rows)


def ride_class_kernel(tile_ref, rows_ref, after_ref, out_ref):
    count = rows_ref.shape[0]
    tile = jnp.broadcast_to(tile_ref[...][None], (count // 8, 8, PIECE)).reshape(count, PIECE)
    ride = (iota(rows_ref.shape, 0) & 7) >= 2
    out_ref[...] = jnp.where(ride, tile, rows_ref[...].astype(F32)).astype(BF16)


def ride_class(tile, rows, after):
    step = 1024
    last = pl.BlockSpec((step, PIECE), lambda i: (i, rows.shape[1] // PIECE - 1))
    return pl.pallas_call(
        ride_class_kernel,
        grid=(rows.shape[0] // step,),
        in_specs=[whole(tile), last, pl.BlockSpec(memory_space=pl.ANY)],
        out_specs=last,
        out_shape=jax.ShapeDtypeStruct(rows.shape, BF16),
        input_output_aliases={1: 0},
        compiler_params=params(16),
        name="ride_class",
    )(tile, rows, after)


def class_rows_kernel(rows_ref, out_ref):
    rows = rows_ref[...]
    shape = out_ref.shape[0], rows.shape[0]
    j, i = iota(shape, 0), iota(shape, 1)
    sender, row, sub = (i >> 3) == (j >> 1), j & 1, i & 7
    first = dot(zero_one(sender & ((sub == 2 + row) | (sub == 4 + row))), rows)
    rest = dot(zero_one(sender & (sub == 6)), rows)
    rest = rest + pltpu.roll(rest, 64, 1)
    odd = (iota(rest.shape, 0) & 1) == 1
    rest = jnp.where(odd, pltpu.roll(rest, 96, 1), rest)
    out_ref[:, :PIECE] = first
    out_ref[:, PIECE:] = rest[:, : out_ref.shape[1] - PIECE]


def class_rows(rows, classes):
    step = 1024
    return pl.pallas_call(
        class_rows_kernel,
        grid=(rows.shape[0] // step,),
        in_specs=[pl.BlockSpec((step, PIECE), lambda i: (i, rows.shape[1] // PIECE - 1))],
        out_specs=pl.BlockSpec((step // 4, classes), lambda i: (i, 0)),
        out_shape=jax.ShapeDtypeStruct((rows.shape[0] // 4, classes), F32),
        compiler_params=params(16),
        name="class_rows",
    )(rows)


def token(rows):
    return rows[:8, :128]


def exchange(rows):
    return lax.all_to_all(rows, BOTH, split_axis=0, concat_axis=0, tiled=True)


def on_device(
    features,
    hidden_weight,
    class_weight,
    req_owner,
    req_block,
    req_offset,
    hop1_counts,
    hop2_counts,
    prior_agg,
    prior_hop1,
    cotangent,
):
    outer, inner = lax.axis_size("gx"), lax.axis_size("gy")
    want, node = route(req_owner.reshape(1, -1), req_block, req_offset, hop2_counts)
    asked = lax.all_to_all(
        lax.all_to_all(
            want.reshape(outer, inner, LANES_CAP), "gx", split_axis=0, concat_axis=0, tiled=True
        ),
        "gy",
        split_axis=1,
        concat_axis=1,
        tiled=True,
    ).reshape(DEVICES, LANES_CAP)
    feat, classes = features.shape[1], class_weight.shape[1]
    nodes = hop2_counts.shape[1]
    first = node[:, :FIRST].reshape(1, -1)
    tail = node[:, FIRST:CAP]
    folded = jnp.concatenate([tail, tail], axis=1).reshape(1, -1)
    last = jnp.pad(node[:, CAP - 2 : CAP], ((0, 0), (0, 6))).reshape(1, -1)

    picked = gather(0, asked, features, token(asked))
    part0 = exchange(picked)
    core = (lax.axis_index("gx") % CORES).reshape(1)
    x = (lax.axis_index("gy") // Y).reshape(1)
    kept, sent = backward(
        core, prior_agg, prior_hop1, cotangent, hidden_weight, class_weight, token(picked)
    )
    own, *sent = split(x, kept, swap(sent, "gx", 1))
    got = [swap(rows, "gy", Y * k) for k, rows in enumerate(sent, 1)]
    picked = ride_sums(own, got, gather(1, asked, features, token(own)))
    part1 = exchange(picked)
    sums = sum_slots(first, part0, nodes)
    picked = gather(2, asked, features, token(picked))
    own, tile = own_sums(part1)
    part2 = exchange(ride_class(tile, picked, token(sums)))
    hidden_grad = own[: 2 * feat // PIECE].reshape(-1, 2, PIECE).transpose(0, 2, 1).reshape(-1, 2)
    pre, sums = sum_folded(folded, part1, sums, hop2_counts, hidden_weight)
    class_grad = class_rows(part2, classes)
    logits = forward(
        first, last, part2, sums, pre, hop1_counts, hop2_counts, hidden_weight, class_weight
    )
    return (logits, hidden_grad, class_grad)


def solution(mesh):
    placed = (
        P(BOTH, None),
        P(),
        P(),
        P(BOTH, None, None),
        P(BOTH, None),
        P(BOTH, None),
        P(BOTH, None),
        P(BOTH, None),
        P(BOTH, None),
        P(BOTH, None),
        P(BOTH, None),
    )
    return jax.shard_map(
        on_device,
        mesh=mesh,
        in_specs=placed,
        out_specs=(P(BOTH, None), P(None, BOTH), P()),
        check_vma=False,
    )
```

```python
import jax
import jax.numpy as jnp
from jax import lax
from jax.experimental import pallas as pl
from jax.experimental.pallas import tpu as pltpu
from jax.sharding import PartitionSpec as P

BLOCK_ROWS = 128
DEVICES = 512
CAP = 12
LANES_CAP = 16
FIRST = 8
PIECE = 128
MOST_MIB = 60
BOTH = ("gx", "gy")
Z, CORES, X, Y = 8, 2, 4, 8
F32 = jnp.float32
BF16 = jnp.bfloat16
MIB = 1 << 20


def iota(shape, dim):
    return lax.broadcasted_iota(jnp.int32, shape, dim)


def dot(a, b, dims=((1,), (0,))):
    return lax.dot_general(a, b, (dims, ((), ())), preferred_element_type=F32)


def params(mib, semantics=("arbitrary",)):
    return pltpu.CompilerParams(dimension_semantics=semantics, vmem_limit_bytes=mib * MIB)


def route_kernel(owner_ref, block_ref, offset_ref, hop2_ref, want_ref, node_ref):
    nodes = hop2_ref.shape[1]
    step = 256
    counts = hop2_ref[...].astype(F32)
    ends = jnp.sum(
        jnp.where(iota((nodes, nodes), 1) <= iota((nodes, nodes), 0), counts, 0.0),
        axis=1,
        keepdims=True,
    )
    before = (iota((step, step), 0) < iota((step, step), 1)).astype(BF16)
    owner_at = iota((DEVICES, step), 0)
    slot_at = iota((LANES_CAP, step), 0)
    carry = jnp.zeros((DEVICES, 1), F32)
    total = jnp.zeros((DEVICES, 2 * LANES_CAP), F32)
    for blk in range(owner_ref.shape[1] // step):
        at = pl.ds(blk * step, step)
        place = blk * step + iota((1, step), 1)
        if blk * step < nodes:
            node = place
        else:
            inside = (place - nodes).astype(F32)
            node = jnp.sum(jnp.where(ends <= inside, 1.0, 0.0), axis=0, keepdims=True).astype(
                jnp.int32
            )
        want = block_ref[:, at] * BLOCK_ROWS + offset_ref[:, at]
        here = owner_at == owner_ref[:, at]
        here_f = jnp.where(here, 1.0, 0.0)
        here_b = here_f.astype(BF16)
        seen = dot(here_b, before) + carry
        rank = jnp.sum(jnp.where(here, seen, 0.0), axis=0, keepdims=True).astype(jnp.int32)
        carry = carry + jnp.sum(here_f, axis=1, keepdims=True)
        mine = slot_at == rank

        def fields(part):
            return jnp.concatenate(
                [
                    jnp.where(mine, part(want + 1).astype(F32), 0.0),
                    jnp.where(mine, part(node + 1).astype(F32), 0.0),
                ],
                axis=0,
            ).astype(BF16)

        total = total + dot(here_b, fields(lambda v: v & ~31), ((1,), (1,)))
        total = total + dot(here_b, fields(lambda v: v & 31), ((1,), (1,)))
    total = total.astype(jnp.int32)
    want_ref[...] = total[:, :LANES_CAP]
    node_ref[...] = total[:, LANES_CAP:]


def route(owners, blocks, offsets, hop2):
    shape = jax.ShapeDtypeStruct((DEVICES, LANES_CAP), jnp.int32)
    return pl.pallas_call(
        route_kernel,
        out_shape=(shape, shape),
        compiler_params=pltpu.CompilerParams(vmem_limit_bytes=MOST_MIB * MIB),
        cost_estimate=pl.CostEstimate(flops=4_000_000_000, bytes_accessed=200_000, transcendentals=0),
        name="route",
    )(owners, blocks, offsets, hop2)


def picks_of(want_ref, held, slot_of):
    readers, lanes = want_ref.shape
    rows = readers * 8
    spread = jnp.broadcast_to(want_ref[...].astype(F32)[:, None, :], (readers, 8, lanes))
    slot = slot_of(iota((readers, 8, lanes), 1))
    chosen = jnp.sum(
        jnp.where(iota((readers, 8, lanes), 2) == slot, spread, 0.0), axis=2, keepdims=True
    )
    chosen = chosen.reshape(rows, 1).astype(jnp.int32) - 1
    return jnp.where(iota((rows, held), 1) == chosen, 1.0, 0.0).astype(BF16)


def gather_kernel(part, want_ref, features_ref, after_ref, out_ref):
    held = features_ref.shape[0]
    if part == 1:
        found = dot(picks_of(want_ref, held, lambda sub: FIRST + (sub & 3)), features_ref[...])
        half = found.shape[1] // 2
        low = (iota((found.shape[0], half), 0) & 7) < 4
        out_ref[...] = jnp.where(low, found[:, :half], found[:, half:]).astype(BF16)
        return
    half = features_ref.shape[1]
    found = dot(picks_of(want_ref, held, lambda sub: sub), features_ref[...])
    out_ref[:, :half] = found.astype(BF16)
    if part == 2:
        last = dot(
            picks_of(want_ref, held, lambda sub: jnp.where(sub < 2, CAP - 2 + sub, LANES_CAP)),
            features_ref[:, half - PIECE :],
        )
        out_ref[:, half:] = last.astype(BF16)


def gather(part, want, features, after):
    held, width = features.shape
    half = width // 2
    sent = half + PIECE if part == 2 else half
    readers = 128
    if part == 1:
        source = pl.BlockSpec((held, width), lambda i: (0, 0))
    else:
        source = pl.BlockSpec((held, half), lambda i: (0, part // 2))
    return pl.pallas_call(
        lambda *refs: gather_kernel(part, *refs),
        grid=(DEVICES // readers,),
        in_specs=[
            pl.BlockSpec((readers, LANES_CAP), lambda i: (i, 0)),
            source,
            pl.BlockSpec(memory_space=pl.ANY),
        ],
        out_specs=pl.BlockSpec((readers * 8, sent), lambda i: (i, 0)),
        out_shape=jax.ShapeDtypeStruct((DEVICES * 8, sent), BF16),
        compiler_params=params(MOST_MIB),
        cost_estimate=pl.CostEstimate(
            flops=2 * DEVICES * 8 * held * (half if part == 0 else width),
            bytes_accessed=DEVICES * 16 * sent,
            transcendentals=0,
        ),
        name=f"gather_{part}",
    )(want, features, after)


def taken(node_ref, nodes):
    return iota((nodes, node_ref.shape[1]), 0) == node_ref[...] - 1


def zero_one(mask):
    return jnp.where(mask, 1.0, 0.0).astype(BF16)


def add_up(out_ref, part):
    @pl.when(pl.program_id(0) == 0)
    def _():
        out_ref[...] = part

    @pl.when(pl.program_id(0) > 0)
    def _():
        out_ref[...] += part


def whole(a):
    return pl.BlockSpec(a.shape, lambda i: (0,) * a.ndim)


def sum_slots_kernel(node_ref, rows_ref, out_ref):
    add_up(out_ref, dot(zero_one(taken(node_ref, out_ref.shape[0])), rows_ref[...]))


def sum_slots(node, rows, nodes):
    step = 1024
    count, half = rows.shape
    return pl.pallas_call(
        sum_slots_kernel,
        grid=(count // step,),
        in_specs=[
            pl.BlockSpec((1, step), lambda i: (0, i)),
            pl.BlockSpec((step, half), lambda i: (i, 0)),
        ],
        out_specs=pl.BlockSpec((nodes, half), lambda i: (0, 0)),
        out_shape=jax.ShapeDtypeStruct((nodes, half), F32),
        compiler_params=params(MOST_MIB),
        cost_estimate=pl.CostEstimate(
            flops=2 * nodes * count * half, bytes_accessed=count * half * 2, transcendentals=0
        ),
        name="sum_slots",
    )(node, rows)


def group_sizes(hop2_ref):
    nodes = hop2_ref.shape[1]
    same = iota((nodes, nodes), 0) == iota((nodes, nodes), 1)
    counts = jnp.where(same, hop2_ref[...].astype(F32), 0.0)
    return 1.0 + jnp.sum(counts, axis=1, keepdims=True)


def sum_folded_kernel(
    node_ref,
    rows_ref,
    sums_ref,
    hop1_ref,
    hop2_ref,
    w1_ref,
    pre_ref,
    high_ref,
    groups_ref,
    sizes1_ref,
    sizes2_ref,
    low_ref,
):
    nodes, half = sums_ref.shape
    takes = taken(node_ref, nodes)
    low = (iota(takes.shape, 1) & 7) < 4
    rows = rows_ref[...]
    ride = rows[:, half - PIECE :].astype(F32)
    ride = jnp.where((iota(ride.shape, 0) & 7) >= 6, 0.0, ride).astype(BF16)
    rows = jnp.concatenate([rows[:, : half - PIECE], ride], axis=1)
    add_up(low_ref, dot(zero_one(takes & low), rows))
    add_up(high_ref, dot(zero_one(takes & jnp.logical_not(low)), rows))

    @pl.when(pl.program_id(0) == pl.num_programs(0) - 1)
    def _():
        sizes2 = group_sizes(hop2_ref)
        sizes2_ref[...] = sizes2
        groups_ref[...], sizes1_ref[...] = seed_groups(hop1_ref[...].astype(F32), nodes)
        agg = ((sums_ref[...] + low_ref[...]) / sizes2).astype(BF16)
        pre_ref[...] = dot(agg, w1_ref[...])


def sum_folded(node, rows, sums, hop1, hop2, w1):
    step = 1024
    count, half = rows.shape
    nodes, hid, seeds = sums.shape[0], w1.shape[1], hop1.shape[1]
    given = [
        jax.ShapeDtypeStruct((nodes, hid), F32),
        jax.ShapeDtypeStruct((nodes, half), F32),
        jax.ShapeDtypeStruct((seeds, nodes), BF16),
        jax.ShapeDtypeStruct((seeds, 1), F32),
        jax.ShapeDtypeStruct((nodes, 1), F32),
    ]
    return pl.pallas_call(
        sum_folded_kernel,
        grid=(count // step,),
        in_specs=[
            pl.BlockSpec((1, step), lambda i: (0, i)),
            pl.BlockSpec((step, half), lambda i: (i, 0)),
            whole(sums),
            whole(hop1),
            whole(hop2),
            pl.BlockSpec((half, hid), lambda i: (0, 0)),
        ],
        out_specs=[whole(a) for a in given],
        out_shape=given,
        scratch_shapes=[pltpu.VMEM((nodes, half), F32)],
        compiler_params=params(MOST_MIB),
        cost_estimate=pl.CostEstimate(
            flops=4 * nodes * count * half, bytes_accessed=count * half * 2, transcendentals=0
        ),
        name="sum_folded",
    )(node, rows, sums, hop1, hop2, w1)


def seed_groups(counts, nodes):
    seeds = counts.shape[1]
    row, col = iota((seeds, seeds), 0), iota((seeds, seeds), 1)
    ends = jnp.sum(jnp.where(col <= row, counts, 0.0), axis=1, keepdims=True)
    own = jnp.sum(jnp.where(col == row, counts, 0.0), axis=1, keepdims=True)
    seed, node = iota((seeds, nodes), 0), iota((seeds, nodes), 1)
    inside = (node - seeds).astype(F32)
    grouped = (node >= seeds) & (inside >= ends - own) & (inside < ends)
    return jnp.where(grouped | (seed == node), 1.0, 0.0).astype(BF16), 1.0 + own


def forward_kernel(
    node_ref,
    last_ref,
    rows_ref,
    sums_ref,
    pre_ref,
    groups_ref,
    sizes1_ref,
    sizes2_ref,
    w1_ref,
    w2_ref,
    out_ref,
    class_ref,
    acc_ref,
    pre_all,
    w1_all,
):
    nodes, half = sums_ref.shape
    block = pre_ref.shape[1]
    pre_all[pl.program_id(0)] = pre_ref[...]
    w1_all[pl.program_id(0)] = w1_ref[...]
    add_up(acc_ref, dot(zero_one(taken(node_ref, nodes)), rows_ref[:, :half]))
    tile = rows_ref[:, half:]
    count = tile.shape[0]
    shape = count // 4, count
    j, i = iota(shape, 0), iota(shape, 1)
    same, odd, sub = (i >> 3) == (j >> 1), j & 1, i & 7
    last = dot(zero_one(same & (sub == odd)), tile).astype(BF16)
    acc_ref[:, half - PIECE :] += dot(zero_one(taken(last_ref, nodes)), last)

    first = zero_one(same & ((sub == 2 + odd) | (sub == 4 + odd)))
    class_ref[:PIECE, :] = dot(tile, first, ((0,), (1,)))
    rest = dot(tile, zero_one(same & (sub == 6)), ((0,), (1,)))
    rest = rest[:64] + rest[64:]
    more = class_ref.shape[0] - PIECE
    odd = (iota((more, count // 4), 1) & 1) == 1
    class_ref[PIECE:, :] = jnp.where(odd, rest[32 : 32 + more], rest[:more])

    @pl.when(pl.program_id(0) == pl.num_programs(0) - 1)
    def _():
        agg_one = ((sums_ref[...] + acc_ref[...]) / sizes2_ref[...]).astype(BF16)
        groups = groups_ref[...]
        scale = 1.0 / sizes1_ref[...]
        total = jnp.zeros(out_ref.shape, F32)
        for k in range(pre_all.shape[0]):
            pre = pre_all[k] + dot(agg_one, w1_all[k])
            hidden = (pre * jax.nn.sigmoid(pre)).astype(BF16)
            agg_two = (dot(groups, hidden) * scale).astype(BF16)
            mine = slice(k * block, (k + 1) * block)
            total = total + dot(w2_ref[:, mine], agg_two, ((1,), (1,)))
        out_ref[...] = total


def forward(node, last, rows, sums, pre, groups, sizes1, sizes2, w1, w2):
    step = 1024
    count, sent = rows.shape
    nodes, half = sums.shape
    hid = w1.shape[1]
    seeds, classes = groups.shape[0], w2.shape[0]
    steps = count // step
    return pl.pallas_call(
        forward_kernel,
        grid=(steps,),
        in_specs=[
            pl.BlockSpec((1, step), lambda i: (0, i)),
            pl.BlockSpec((1, step // 4), lambda i: (0, i)),
            pl.BlockSpec((step, sent), lambda i: (i, 0)),
            whole(sums),
            pl.BlockSpec((nodes, hid // steps), lambda i: (0, i)),
            whole(groups),
            whole(sizes1),
            whole(sizes2),
            pl.BlockSpec((half, hid // steps), lambda i: (1, i)),
            whole(w2),
        ],
        out_specs=[
            pl.BlockSpec((classes, seeds), lambda i: (0, 0)),
            pl.BlockSpec((classes, step // 4), lambda i: (0, i)),
        ],
        out_shape=[
            jax.ShapeDtypeStruct((classes, seeds), F32),
            jax.ShapeDtypeStruct((classes, count // 4), F32),
        ],
        scratch_shapes=[
            pltpu.VMEM((nodes, half), F32),
            pltpu.VMEM((steps, nodes, hid // steps), F32),
            pltpu.VMEM((steps, half, hid // steps), BF16),
        ],
        compiler_params=params(MOST_MIB),
        cost_estimate=pl.CostEstimate(
            flops=2 * nodes * count * half + 2 * nodes * half * hid,
            bytes_accessed=count * sent * 2,
            transcendentals=nodes * hid,
        ),
        name="forward",
    )(node, last, rows, sums, pre, groups, sizes1, sizes2, w1, w2)


def backward_kernel(
    core_ref, agg_ref, hop1_ref, cot_ref, w1_ref, w2_ref, after_ref, kept_ref, sent_ref
):
    nodes = agg_ref.shape[0]
    seeds = hop1_ref.shape[1]
    counts = hop1_ref[...].astype(F32)
    groups, sizes = seed_groups(counts, nodes)
    scale = 1.0 / sizes
    row, col = iota((seeds, seeds), 0), iota((seeds, seeds), 1)
    own = sizes - 1.0
    ends = jnp.sum(jnp.where(row <= col, own, 0.0), axis=0, keepdims=True)
    node, seed = iota((nodes, seeds), 0), iota((nodes, seeds), 1)
    inside = (node - seeds).astype(F32)
    grouped = (node >= seeds) & (inside >= ends - counts) & (inside < ends)
    hands = grouped | (seed == node)
    node_scale = jnp.sum(jnp.where(hands, 1.0 / (1.0 + counts), 0.0), axis=1, keepdims=True)
    cot = cot_ref[...]
    node_cot = dot(zero_one(hands), cot, ((1,), (1,))).astype(BF16)

    agg = agg_ref[...]
    pre = dot(agg, w1_ref[...])
    sigma = jax.nn.sigmoid(pre)
    hidden = (pre * sigma).astype(BF16)
    agg_two = (dot(groups, hidden) * scale).astype(BF16)
    classes = cot.shape[0]
    wide = zero_one(iota((2 * PIECE, classes), 0) == iota((2 * PIECE, classes), 1))
    class_term = dot(agg_two, dot(wide, cot).astype(BF16), ((0,), (1,)))
    d_hidden = dot(node_cot, w2_ref[...]) * node_scale
    d_pre = (d_hidden * sigma * (1.0 + pre * (1.0 - sigma))).astype(BF16)
    hidden_term = dot(d_pre, agg, ((0,), (0,)))
    first = core_ref[0] == 0
    half = kept_ref.shape[1] // 2
    mine = slice(0, half), slice(half, 2 * half)
    low = hidden_term[:, :half], hidden_term[:, half : 2 * half]
    high = hidden_term[:, 2 * half :], class_term
    for at, a, b in zip(mine, low, high):
        kept_ref[:, at] = jnp.where(first, a, b)
        sent_ref[:, at] = jnp.where(first, b, a)


def backward(core, agg, hop1, cot, w1, w2, after):
    nodes, feat = agg.shape
    hid = w1.shape[1]
    classes = cot.shape[0]
    step = 256
    half = (feat + 2 * PIECE) // 2
    return pl.pallas_call(
        backward_kernel,
        grid=(hid // step,),
        in_specs=[
            pl.BlockSpec(memory_space=pltpu.SMEM),
            whole(agg),
            whole(hop1),
            whole(cot),
            pl.BlockSpec((feat, step), lambda i: (0, i)),
            pl.BlockSpec((classes, step), lambda i: (0, i)),
            pl.BlockSpec(memory_space=pl.ANY),
        ],
        out_specs=[pl.BlockSpec((step, half), lambda i: (i, 0))] * 2,
        out_shape=[jax.ShapeDtypeStruct((hid, half), F32)] * 2,
        compiler_params=params(MOST_MIB),
        cost_estimate=pl.CostEstimate(
            flops=4 * nodes * feat * hid, bytes_accessed=6 * MIB, transcendentals=nodes * hid
        ),
        name="backward",
    )(core, agg, hop1, cot, w1, w2, after)


def swap(rows, axis, bit):
    size = lax.axis_size(axis)
    return lax.ppermute(rows, axis, [(i, i ^ bit) for i in range(size)])


def split_kernel(x_ref, kept_ref, got_ref, own_ref, *sent_refs):
    def piece(k):
        at = pl.ds(pl.multiple_of(k * PIECE, PIECE), PIECE)
        return kept_ref[:, at] + got_ref[:, at]

    x = x_ref[0]
    own_ref[...] = piece(x)
    for k, ref in enumerate(sent_refs, 1):
        ref[...] = piece(x ^ k).astype(BF16)


def split(x, kept, got):
    rows, width = kept.shape
    step = 256
    block = pl.BlockSpec((step, width), lambda i: (i, 0))
    return pl.pallas_call(
        split_kernel,
        grid=(rows // step,),
        in_specs=[pl.BlockSpec(memory_space=pltpu.SMEM), block, block],
        out_specs=[pl.BlockSpec((step, PIECE), lambda i: (i, 0))] * X,
        out_shape=[jax.ShapeDtypeStruct((rows, PIECE), F32)]
        + [jax.ShapeDtypeStruct((rows, PIECE), BF16)] * (X - 1),
        compiler_params=params(MOST_MIB),
        name="split",
    )(x, kept, got)


def ride_sums_kernel(own_ref, *refs):
    got, rows_ref, out_ref = refs[: X - 1], refs[X - 1], refs[X]
    piece = own_ref[...]
    for ref in got:
        piece = piece + ref[...].astype(F32)
    shape = rows_ref.shape[0], piece.shape[0]
    i, j = iota(shape, 0), iota(shape, 1)
    put = dot(zero_one(((i >> 3) == (j >> 1)) & ((i & 7) == 6 + (j & 1))), piece.astype(BF16))
    ride = (iota(rows_ref.shape, 0) & 7) >= 6
    out_ref[...] = jnp.where(ride, put, rows_ref[...].astype(F32)).astype(BF16)


def ride_sums(own, got, rows):
    readers = 64
    mine = pl.BlockSpec((readers * 2, PIECE), lambda i: (i, 0))
    tile = pl.BlockSpec((readers * 8, PIECE), lambda i: (i, rows.shape[1] // PIECE - 1))
    return pl.pallas_call(
        ride_sums_kernel,
        grid=(DEVICES // readers,),
        in_specs=[mine] * X + [tile],
        out_specs=tile,
        out_shape=jax.ShapeDtypeStruct(rows.shape, BF16),
        input_output_aliases={X: 0},
        compiler_params=params(16),
        name="ride_sums",
    )(own, *got, rows)


def own_sums_kernel(rows_ref, out_ref, tile_ref):
    count = rows_ref.shape[0]
    shape = out_ref.shape[0], count
    j, i = iota(shape, 0), pl.program_id(0) * count + iota(shape, 1)
    add_up(out_ref, dot(zero_one((((i >> 6) & 7) == (j >> 1)) & ((i & 7) == 6 + (j & 1))), rows_ref[...]))

    @pl.when(pl.program_id(0) == pl.num_programs(0) - 1)
    def _():
        total = out_ref[...]
        high = total.astype(BF16).astype(F32)
        low = total - high
        tile_ref[...] = jnp.zeros(tile_ref.shape, F32)
        tile_ref[2:4, :] = high[12:14]
        tile_ref[4:6, :] = low[12:14]
        tile_ref[6:7, :] = (
            high[14:15]
            + pltpu.roll(high[15:16], 32, 1)
            + pltpu.roll(low[14:15], 64, 1)
            + pltpu.roll(low[15:16], 96, 1)
        )


def own_sums(rows):
    step = 2048
    return pl.pallas_call(
        own_sums_kernel,
        grid=(rows.shape[0] // step,),
        in_specs=[pl.BlockSpec((step, PIECE), lambda i: (i, rows.shape[1] // PIECE - 1))],
        out_specs=[
            pl.BlockSpec((16, PIECE), lambda i: (0, 0)),
            pl.BlockSpec((8, PIECE), lambda i: (0, 0)),
        ],
        out_shape=[
            jax.ShapeDtypeStruct((16, PIECE), F32),
            jax.ShapeDtypeStruct((8, PIECE), F32),
        ],
        compiler_params=params(16),
        name="own_sums",
    )(rows)


def ride_class_kernel(tile_ref, rows_ref, after_ref, out_ref):
    count = rows_ref.shape[0]
    tile = jnp.broadcast_to(tile_ref[...][None], (count // 8, 8, PIECE)).reshape(count, PIECE)
    ride = (iota(rows_ref.shape, 0) & 7) >= 2
    out_ref[...] = jnp.where(ride, tile, rows_ref[...].astype(F32)).astype(BF16)


def ride_class(tile, rows, after):
    step = 4096
    last = pl.BlockSpec((step, PIECE), lambda i: (i, rows.shape[1] // PIECE - 1))
    return pl.pallas_call(
        ride_class_kernel,
        grid=(rows.shape[0] // step,),
        in_specs=[whole(tile), last, pl.BlockSpec(memory_space=pl.ANY)],
        out_specs=last,
        out_shape=jax.ShapeDtypeStruct(rows.shape, BF16),
        input_output_aliases={1: 0},
        compiler_params=params(MOST_MIB),
        name="ride_class",
    )(tile, rows, after)


def token(rows):
    return rows[:8, :128]


def exchange(rows):
    return lax.all_to_all(rows, BOTH, split_axis=0, concat_axis=0, tiled=True)


def on_device(
    features,
    hidden_weight,
    class_weight,
    req_owner,
    req_block,
    req_offset,
    hop1_counts,
    hop2_counts,
    prior_agg,
    prior_hop1,
    cotangent,
):
    outer, inner = lax.axis_size("gx"), lax.axis_size("gy")
    want, node = route(req_owner.reshape(1, -1), req_block, req_offset, hop2_counts)
    asked = lax.all_to_all(
        lax.all_to_all(
            want.reshape(outer, inner, LANES_CAP), "gx", split_axis=0, concat_axis=0, tiled=True
        ),
        "gy",
        split_axis=1,
        concat_axis=1,
        tiled=True,
    ).reshape(DEVICES, LANES_CAP)
    feat = features.shape[1]
    nodes = hop2_counts.shape[1]
    first = node[:, :FIRST].reshape(1, -1)
    tail = node[:, FIRST:CAP]
    folded = jnp.concatenate([tail, tail], axis=1).reshape(1, -1)
    last = node[:, CAP - 2 : CAP].reshape(1, -1)
    w2 = class_weight.T

    picked = gather(0, asked, features, asked)
    part0 = exchange(picked)
    core = (lax.axis_index("gx") % CORES).reshape(1)
    x = (lax.axis_index("gy") // Y).reshape(1)
    kept, sent = backward(
        core, prior_agg, prior_hop1, cotangent.T, hidden_weight, w2, token(picked)
    )
    own, *sent = split(x, kept, swap(sent, "gx", 1))
    got = [swap(rows, "gy", Y * k) for k, rows in enumerate(sent, 1)]
    picked = ride_sums(own, got, gather(1, asked, features, token(own)))
    part1 = exchange(picked)
    sums = sum_slots(first, part0, nodes)
    picked = gather(2, asked, features, token(picked))
    own, tile = own_sums(part1)
    part2 = exchange(ride_class(tile, picked, token(sums)))
    hidden_grad = own[: 2 * feat // PIECE].reshape(-1, 2, PIECE).transpose(1, 0, 2).reshape(2, -1).T
    pre, sums, *groups = sum_folded(
        folded, part1, sums, hop1_counts, hop2_counts, hidden_weight
    )
    logits, class_grad = forward(
        first, last, part2, sums, pre, *groups, hidden_weight, w2
    )
    logits, class_grad = logits.T, class_grad.T
    return (logits, hidden_grad, class_grad)


def solution(mesh):
    placed = (
        P(BOTH, None),
        P(),
        P(),
        P(BOTH, None, None),
        P(BOTH, None),
        P(BOTH, None),
        P(BOTH, None),
        P(BOTH, None),
        P(BOTH, None),
        P(BOTH, None),
        P(BOTH, None),
    )
    return jax.shard_map(
        on_device,
        mesh=mesh,
        in_specs=placed,
        out_specs=(P(BOTH, None), P(None, BOTH), P()),
        check_vma=False,
    )
```

```python
import jax
import jax.numpy as jnp
from jax import lax
from jax.experimental import pallas as pl
from jax.experimental.pallas import tpu as pltpu
from jax.sharding import PartitionSpec as P

BLOCK_ROWS = 128
DEVICES = 512
CAP = 12
LANES_CAP = 16
FIRST = 8
PIECE = 128
MOST_MIB = 60
BOTH = ("gx", "gy")
Z, CORES, X, Y = 8, 2, 4, 8
F32 = jnp.float32
BF16 = jnp.bfloat16
MIB = 1 << 20


def iota(shape, dim):
    return lax.broadcasted_iota(jnp.int32, shape, dim)


def dot(a, b, dims=((1,), (0,))):
    return lax.dot_general(a, b, (dims, ((), ())), preferred_element_type=F32)


def params(mib, semantics=("arbitrary",)):
    return pltpu.CompilerParams(dimension_semantics=semantics, vmem_limit_bytes=mib * MIB)


def route_kernel(owner_ref, block_ref, offset_ref, hop2_ref, want_ref, node_ref):
    nodes = hop2_ref.shape[1]
    step = 256
    counts = hop2_ref[...].astype(F32)
    ends = jnp.sum(
        jnp.where(iota((nodes, nodes), 1) <= iota((nodes, nodes), 0), counts, 0.0),
        axis=1,
        keepdims=True,
    )
    before = (iota((step, step), 0) < iota((step, step), 1)).astype(BF16)
    owner_at = iota((DEVICES, step), 0)
    slot_at = iota((LANES_CAP, step), 0)
    ones = jnp.ones((step, step), BF16)
    carry = jnp.zeros((DEVICES, step), F32)
    total = jnp.zeros((DEVICES, 2 * LANES_CAP), F32)
    for blk in range(owner_ref.shape[1] // step):
        at = pl.ds(blk * step, step)
        place = blk * step + iota((1, step), 1)
        if blk * step < nodes:
            node = place
        else:
            inside = (place - nodes).astype(F32)
            node = jnp.sum(jnp.where(ends <= inside, 1.0, 0.0), axis=0, keepdims=True).astype(
                jnp.int32
            )
        want = block_ref[:, at] * BLOCK_ROWS + offset_ref[:, at]
        here = owner_at == owner_ref[:, at]
        here_b = jnp.where(here, 1.0, 0.0).astype(BF16)
        seen = dot(here_b, before) + carry
        rank = jnp.sum(jnp.where(here, seen, 0.0), axis=0, keepdims=True).astype(jnp.int32)
        carry = carry + dot(here_b, ones)
        mine = slot_at == rank

        def fields(part):
            return jnp.concatenate(
                [
                    jnp.where(mine, part(want + 1).astype(F32), 0.0),
                    jnp.where(mine, part(node + 1).astype(F32), 0.0),
                ],
                axis=0,
            ).astype(BF16)

        total = total + dot(here_b, fields(lambda v: v & ~31), ((1,), (1,)))
        total = total + dot(here_b, fields(lambda v: v & 31), ((1,), (1,)))
    total = total.astype(jnp.int32)
    want_ref[...] = total[:, :LANES_CAP]
    node_ref[...] = total[:, LANES_CAP:]


def route(owners, blocks, offsets, hop2):
    shape = jax.ShapeDtypeStruct((DEVICES, LANES_CAP), jnp.int32)
    return pl.pallas_call(
        route_kernel,
        out_shape=(shape, shape),
        compiler_params=pltpu.CompilerParams(vmem_limit_bytes=MOST_MIB * MIB),
        cost_estimate=pl.CostEstimate(flops=4_000_000_000, bytes_accessed=200_000, transcendentals=0),
        name="route",
    )(owners, blocks, offsets, hop2)


def picks_of(want_ref, held, slot_of):
    readers, lanes = want_ref.shape
    rows = readers * 8
    spread = jnp.broadcast_to(want_ref[...].astype(F32)[:, None, :], (readers, 8, lanes))
    slot = slot_of(iota((readers, 8, lanes), 1))
    chosen = jnp.sum(
        jnp.where(iota((readers, 8, lanes), 2) == slot, spread, 0.0), axis=2, keepdims=True
    )
    chosen = chosen.reshape(rows, 1).astype(jnp.int32) - 1
    return jnp.where(iota((rows, held), 1) == chosen, 1.0, 0.0).astype(BF16)


def gather_kernel(part, want_ref, features_ref, after_ref, out_ref):
    held = features_ref.shape[0]
    if part == 1:
        found = dot(picks_of(want_ref, held, lambda sub: FIRST + (sub & 3)), features_ref[...])
        half = found.shape[1] // 2
        low = (iota((found.shape[0], half), 0) & 7) < 4
        out_ref[...] = jnp.where(low, found[:, :half], found[:, half:]).astype(BF16)
        return
    half = features_ref.shape[1]
    found = dot(picks_of(want_ref, held, lambda sub: sub), features_ref[...])
    out_ref[:, :half] = found.astype(BF16)
    if part == 2:
        last = dot(
            picks_of(want_ref, held, lambda sub: jnp.where(sub < 2, CAP - 2 + sub, LANES_CAP)),
            features_ref[:, half - PIECE :],
        )
        out_ref[:, half:] = last.astype(BF16)


def gather(part, want, features, after):
    held, width = features.shape
    half = width // 2
    sent = half + PIECE if part == 2 else half
    readers = 128
    if part == 1:
        source = pl.BlockSpec((held, width), lambda i: (0, 0))
    else:
        source = pl.BlockSpec((held, half), lambda i: (0, part // 2))
    return pl.pallas_call(
        lambda *refs: gather_kernel(part, *refs),
        grid=(DEVICES // readers,),
        in_specs=[
            pl.BlockSpec((readers, LANES_CAP), lambda i: (i, 0)),
            source,
            pl.BlockSpec(memory_space=pl.ANY),
        ],
        out_specs=pl.BlockSpec((readers * 8, sent), lambda i: (i, 0)),
        out_shape=jax.ShapeDtypeStruct((DEVICES * 8, sent), BF16),
        compiler_params=params(MOST_MIB),
        cost_estimate=pl.CostEstimate(
            flops=2 * DEVICES * 8 * held * (half if part == 0 else width),
            bytes_accessed=DEVICES * 16 * sent,
            transcendentals=0,
        ),
        name=f"gather_{part}",
    )(want, features, after)


def taken(node_ref, nodes):
    return iota((nodes, node_ref.shape[1]), 0) == node_ref[...] - 1


def zero_one(mask):
    return jnp.where(mask, 1.0, 0.0).astype(BF16)


def add_up(out_ref, part):
    @pl.when(pl.program_id(0) == 0)
    def _():
        out_ref[...] = part

    @pl.when(pl.program_id(0) > 0)
    def _():
        out_ref[...] += part


def whole(a):
    return pl.BlockSpec(a.shape, lambda i: (0,) * a.ndim)


def sum_slots_kernel(node_ref, rows_ref, out_ref):
    add_up(out_ref, dot(zero_one(taken(node_ref, out_ref.shape[0])), rows_ref[...]))


def sum_slots(node, rows, nodes):
    step = 1024
    count, half = rows.shape
    return pl.pallas_call(
        sum_slots_kernel,
        grid=(count // step,),
        in_specs=[
            pl.BlockSpec((1, step), lambda i: (0, i)),
            pl.BlockSpec((step, half), lambda i: (i, 0)),
        ],
        out_specs=pl.BlockSpec((nodes, half), lambda i: (0, 0)),
        out_shape=jax.ShapeDtypeStruct((nodes, half), F32),
        compiler_params=params(MOST_MIB),
        cost_estimate=pl.CostEstimate(
            flops=2 * nodes * count * half, bytes_accessed=count * half * 2, transcendentals=0
        ),
        name="sum_slots",
    )(node, rows)


def group_sizes(hop2_ref):
    nodes = hop2_ref.shape[1]
    same = iota((nodes, nodes), 0) == iota((nodes, nodes), 1)
    counts = jnp.where(same, hop2_ref[...].astype(F32), 0.0)
    return 1.0 + jnp.sum(counts, axis=1, keepdims=True)


def sum_folded_kernel(
    node_ref,
    rows_ref,
    sums_ref,
    hop1_ref,
    hop2_ref,
    w1_ref,
    pre_ref,
    high_ref,
    groups_ref,
    sizes1_ref,
    sizes2_ref,
    low_ref,
):
    nodes, half = sums_ref.shape
    takes = taken(node_ref, nodes)
    low = (iota(takes.shape, 1) & 7) < 4
    rows = rows_ref[...]
    ride = rows[:, half - PIECE :].astype(F32)
    ride = jnp.where((iota(ride.shape, 0) & 7) >= 6, 0.0, ride).astype(BF16)
    rows = jnp.concatenate([rows[:, : half - PIECE], ride], axis=1)
    add_up(low_ref, dot(zero_one(takes & low), rows))
    add_up(high_ref, dot(zero_one(takes & jnp.logical_not(low)), rows))

    @pl.when(pl.program_id(0) == pl.num_programs(0) - 1)
    def _():
        sizes2 = group_sizes(hop2_ref)
        sizes2_ref[...] = sizes2
        groups_ref[...], sizes1_ref[...] = seed_groups(hop1_ref[...].astype(F32), nodes)
        agg = ((sums_ref[...] + low_ref[...]) / sizes2).astype(BF16)
        pre_ref[...] = dot(agg, w1_ref[...])


def sum_folded(node, rows, sums, hop1, hop2, w1):
    step = 1024
    count, half = rows.shape
    nodes, hid, seeds = sums.shape[0], w1.shape[1], hop1.shape[1]
    given = [
        jax.ShapeDtypeStruct((nodes, hid), F32),
        jax.ShapeDtypeStruct((nodes, half), F32),
        jax.ShapeDtypeStruct((seeds, nodes), BF16),
        jax.ShapeDtypeStruct((seeds, 1), F32),
        jax.ShapeDtypeStruct((nodes, 1), F32),
    ]
    return pl.pallas_call(
        sum_folded_kernel,
        grid=(count // step,),
        in_specs=[
            pl.BlockSpec((1, step), lambda i: (0, i)),
            pl.BlockSpec((step, half), lambda i: (i, 0)),
            whole(sums),
            whole(hop1),
            whole(hop2),
            pl.BlockSpec((half, hid), lambda i: (0, 0)),
        ],
        out_specs=[whole(a) for a in given],
        out_shape=given,
        scratch_shapes=[pltpu.VMEM((nodes, half), F32)],
        compiler_params=params(MOST_MIB),
        cost_estimate=pl.CostEstimate(
            flops=4 * nodes * count * half, bytes_accessed=count * half * 2, transcendentals=0
        ),
        name="sum_folded",
    )(node, rows, sums, hop1, hop2, w1)


def seed_groups(counts, nodes):
    seeds = counts.shape[1]
    row, col = iota((seeds, seeds), 0), iota((seeds, seeds), 1)
    ends = jnp.sum(jnp.where(col <= row, counts, 0.0), axis=1, keepdims=True)
    own = jnp.sum(jnp.where(col == row, counts, 0.0), axis=1, keepdims=True)
    seed, node = iota((seeds, nodes), 0), iota((seeds, nodes), 1)
    inside = (node - seeds).astype(F32)
    grouped = (node >= seeds) & (inside >= ends - own) & (inside < ends)
    return jnp.where(grouped | (seed == node), 1.0, 0.0).astype(BF16), 1.0 + own


def forward_kernel(
    node_ref,
    last_ref,
    rows_ref,
    sums_ref,
    pre_ref,
    groups_ref,
    sizes1_ref,
    sizes2_ref,
    w1_ref,
    w2_ref,
    out_ref,
    class_ref,
    acc_ref,
    pre_all,
    w1_all,
    takes_ref,
):
    nodes, half = sums_ref.shape
    block = pre_ref.shape[1]
    pre_all[pl.program_id(0)] = pre_ref[...]
    w1_all[pl.program_id(0)] = w1_ref[...]
    add_up(acc_ref, dot(zero_one(taken(node_ref, nodes)), rows_ref[:, :half]))
    tile = rows_ref[:, half:]
    count = tile.shape[0]

    @pl.when(pl.program_id(0) == 0)
    def _():
        shape = count // 4, count
        j, i = iota(shape, 0), iota(shape, 1)
        same, odd, sub = (i >> 3) == (j >> 1), j & 1, i & 7
        takes_ref[0] = zero_one(same & (sub == odd))
        takes_ref[1] = zero_one(same & ((sub == 2 + odd) | (sub == 4 + odd)))
        takes_ref[2] = zero_one(same & (sub == 6))

    last = dot(takes_ref[0], tile).astype(BF16)
    acc_ref[:, half - PIECE :] += dot(zero_one(taken(last_ref, nodes)), last)

    class_ref[:PIECE, :] = dot(tile, takes_ref[1], ((0,), (1,)))
    rest = dot(tile, takes_ref[2], ((0,), (1,)))
    rest = rest[:64] + rest[64:]
    more = class_ref.shape[0] - PIECE
    odd = (iota((more, count // 4), 1) & 1) == 1
    class_ref[PIECE:, :] = jnp.where(odd, rest[32 : 32 + more], rest[:more])

    @pl.when(pl.program_id(0) == pl.num_programs(0) - 1)
    def _():
        agg_one = ((sums_ref[...] + acc_ref[...]) / sizes2_ref[...]).astype(BF16)
        groups = groups_ref[...]
        scale = 1.0 / sizes1_ref[...]
        total = jnp.zeros(out_ref.shape, F32)
        for k in range(pre_all.shape[0]):
            pre = pre_all[k] + dot(agg_one, w1_all[k])
            hidden = (pre * jax.nn.sigmoid(pre)).astype(BF16)
            agg_two = (dot(groups, hidden) * scale).astype(BF16)
            mine = slice(k * block, (k + 1) * block)
            total = total + dot(w2_ref[:, mine], agg_two, ((1,), (1,)))
        out_ref[...] = total


def forward(node, last, rows, sums, pre, groups, sizes1, sizes2, w1, w2):
    step = 1024
    count, sent = rows.shape
    nodes, half = sums.shape
    hid = w1.shape[1]
    seeds, classes = groups.shape[0], w2.shape[0]
    steps = count // step
    return pl.pallas_call(
        forward_kernel,
        grid=(steps,),
        in_specs=[
            pl.BlockSpec((1, step), lambda i: (0, i)),
            pl.BlockSpec((1, step // 4), lambda i: (0, i)),
            pl.BlockSpec((step, sent), lambda i: (i, 0)),
            whole(sums),
            pl.BlockSpec((nodes, hid // steps), lambda i: (0, i)),
            whole(groups),
            whole(sizes1),
            whole(sizes2),
            pl.BlockSpec((half, hid // steps), lambda i: (1, i)),
            whole(w2),
        ],
        out_specs=[
            pl.BlockSpec((classes, seeds), lambda i: (0, 0)),
            pl.BlockSpec((classes, step // 4), lambda i: (0, i)),
        ],
        out_shape=[
            jax.ShapeDtypeStruct((classes, seeds), F32),
            jax.ShapeDtypeStruct((classes, count // 4), F32),
        ],
        scratch_shapes=[
            pltpu.VMEM((nodes, half), F32),
            pltpu.VMEM((steps, nodes, hid // steps), F32),
            pltpu.VMEM((steps, half, hid // steps), BF16),
            pltpu.VMEM((3, step // 4, step), BF16),
        ],
        compiler_params=params(MOST_MIB),
        cost_estimate=pl.CostEstimate(
            flops=2 * nodes * count * half + 2 * nodes * half * hid,
            bytes_accessed=count * sent * 2,
            transcendentals=nodes * hid,
        ),
        name="forward",
    )(node, last, rows, sums, pre, groups, sizes1, sizes2, w1, w2)


def backward_kernel(
    core_ref, agg_ref, hop1_ref, cot_ref, w1_ref, w2_ref, after_ref, kept_ref, sent_ref
):
    nodes = agg_ref.shape[0]
    seeds = hop1_ref.shape[1]
    counts = hop1_ref[...].astype(F32)
    groups, sizes = seed_groups(counts, nodes)
    scale = 1.0 / sizes
    row, col = iota((seeds, seeds), 0), iota((seeds, seeds), 1)
    own = sizes - 1.0
    ends = jnp.sum(jnp.where(row <= col, own, 0.0), axis=0, keepdims=True)
    node, seed = iota((nodes, seeds), 0), iota((nodes, seeds), 1)
    inside = (node - seeds).astype(F32)
    grouped = (node >= seeds) & (inside >= ends - counts) & (inside < ends)
    hands = grouped | (seed == node)
    node_scale = jnp.sum(jnp.where(hands, 1.0 / (1.0 + counts), 0.0), axis=1, keepdims=True)
    cot = cot_ref[...]
    node_cot = dot(zero_one(hands), cot, ((1,), (1,))).astype(BF16)

    agg = agg_ref[...]
    pre = dot(agg, w1_ref[...])
    sigma = jax.nn.sigmoid(pre)
    hidden = (pre * sigma).astype(BF16)
    agg_two = (dot(groups, hidden) * scale).astype(BF16)
    classes = cot.shape[0]
    wide = zero_one(iota((2 * PIECE, classes), 0) == iota((2 * PIECE, classes), 1))
    class_term = dot(agg_two, dot(wide, cot).astype(BF16), ((0,), (1,)))
    d_hidden = dot(node_cot, w2_ref[...]) * node_scale
    d_pre = (d_hidden * sigma * (1.0 + pre * (1.0 - sigma))).astype(BF16)
    hidden_term = dot(d_pre, agg, ((0,), (0,)))
    first = core_ref[0] == 0
    half = kept_ref.shape[1] // 2
    mine = slice(0, half), slice(half, 2 * half)
    low = hidden_term[:, :half], hidden_term[:, half : 2 * half]
    high = hidden_term[:, 2 * half :], class_term
    for at, a, b in zip(mine, low, high):
        kept_ref[:, at] = jnp.where(first, a, b)
        sent_ref[:, at] = jnp.where(first, b, a)


def backward(core, agg, hop1, cot, w1, w2, after):
    nodes, feat = agg.shape
    hid = w1.shape[1]
    classes = cot.shape[0]
    step = 256
    half = (feat + 2 * PIECE) // 2
    return pl.pallas_call(
        backward_kernel,
        grid=(hid // step,),
        in_specs=[
            pl.BlockSpec(memory_space=pltpu.SMEM),
            whole(agg),
            whole(hop1),
            whole(cot),
            pl.BlockSpec((feat, step), lambda i: (0, i)),
            pl.BlockSpec((classes, step), lambda i: (0, i)),
            pl.BlockSpec(memory_space=pl.ANY),
        ],
        out_specs=[pl.BlockSpec((step, half), lambda i: (i, 0))] * 2,
        out_shape=[jax.ShapeDtypeStruct((hid, half), F32)] * 2,
        compiler_params=params(MOST_MIB),
        cost_estimate=pl.CostEstimate(
            flops=4 * nodes * feat * hid, bytes_accessed=6 * MIB, transcendentals=nodes * hid
        ),
        name="backward",
    )(core, agg, hop1, cot, w1, w2, after)


def swap(rows, axis, bit):
    size = lax.axis_size(axis)
    return lax.ppermute(rows, axis, [(i, i ^ bit) for i in range(size)])


def split_kernel(x_ref, kept_ref, got_ref, own_ref, *sent_refs):
    def piece(k):
        at = pl.ds(pl.multiple_of(k * PIECE, PIECE), PIECE)
        return kept_ref[:, at] + got_ref[:, at]

    x = x_ref[0]
    own_ref[...] = piece(x)
    for k, ref in enumerate(sent_refs, 1):
        ref[...] = piece(x ^ k).astype(BF16)


def split(x, kept, got):
    rows, width = kept.shape
    step = 256
    block = pl.BlockSpec((step, width), lambda i: (i, 0))
    return pl.pallas_call(
        split_kernel,
        grid=(rows // step,),
        in_specs=[pl.BlockSpec(memory_space=pltpu.SMEM), block, block],
        out_specs=[pl.BlockSpec((step, PIECE), lambda i: (i, 0))] * X,
        out_shape=[jax.ShapeDtypeStruct((rows, PIECE), F32)]
        + [jax.ShapeDtypeStruct((rows, PIECE), BF16)] * (X - 1),
        compiler_params=params(MOST_MIB),
        name="split",
    )(x, kept, got)


def ride_sums_kernel(own_ref, *refs):
    got, rows_ref, out_ref = refs[: X - 1], refs[X - 1], refs[X]
    piece = own_ref[...]
    for ref in got:
        piece = piece + ref[...].astype(F32)
    shape = rows_ref.shape[0], piece.shape[0]
    i, j = iota(shape, 0), iota(shape, 1)
    put = dot(zero_one(((i >> 3) == (j >> 1)) & ((i & 7) == 6 + (j & 1))), piece.astype(BF16))
    ride = (iota(rows_ref.shape, 0) & 7) >= 6
    out_ref[...] = jnp.where(ride, put, rows_ref[...].astype(F32)).astype(BF16)


def ride_sums(own, got, rows):
    readers = 64
    mine = pl.BlockSpec((readers * 2, PIECE), lambda i: (i, 0))
    tile = pl.BlockSpec((readers * 8, PIECE), lambda i: (i, rows.shape[1] // PIECE - 1))
    return pl.pallas_call(
        ride_sums_kernel,
        grid=(DEVICES // readers,),
        in_specs=[mine] * X + [tile],
        out_specs=tile,
        out_shape=jax.ShapeDtypeStruct(rows.shape, BF16),
        input_output_aliases={X: 0},
        compiler_params=params(16),
        name="ride_sums",
    )(own, *got, rows)


def own_sums_kernel(rows_ref, out_ref, tile_ref):
    count = rows_ref.shape[0]
    shape = out_ref.shape[0], count
    j, i = iota(shape, 0), pl.program_id(0) * count + iota(shape, 1)
    add_up(out_ref, dot(zero_one((((i >> 6) & 7) == (j >> 1)) & ((i & 7) == 6 + (j & 1))), rows_ref[...]))

    @pl.when(pl.program_id(0) == pl.num_programs(0) - 1)
    def _():
        total = out_ref[...]
        high = total.astype(BF16).astype(F32)
        low = total - high
        tile_ref[...] = jnp.zeros(tile_ref.shape, F32)
        tile_ref[2:4, :] = high[12:14]
        tile_ref[4:6, :] = low[12:14]
        tile_ref[6:7, :] = (
            high[14:15]
            + pltpu.roll(high[15:16], 32, 1)
            + pltpu.roll(low[14:15], 64, 1)
            + pltpu.roll(low[15:16], 96, 1)
        )


def own_sums(rows):
    step = 2048
    return pl.pallas_call(
        own_sums_kernel,
        grid=(rows.shape[0] // step,),
        in_specs=[pl.BlockSpec((step, PIECE), lambda i: (i, rows.shape[1] // PIECE - 1))],
        out_specs=[
            pl.BlockSpec((16, PIECE), lambda i: (0, 0)),
            pl.BlockSpec((8, PIECE), lambda i: (0, 0)),
        ],
        out_shape=[
            jax.ShapeDtypeStruct((16, PIECE), F32),
            jax.ShapeDtypeStruct((8, PIECE), F32),
        ],
        compiler_params=params(16),
        name="own_sums",
    )(rows)


def ride_class_kernel(tile_ref, rows_ref, after_ref, out_ref):
    count = rows_ref.shape[0]
    tile = jnp.broadcast_to(tile_ref[...][None], (count // 8, 8, PIECE)).reshape(count, PIECE)
    ride = (iota(rows_ref.shape, 0) & 7) >= 2
    out_ref[...] = jnp.where(ride, tile, rows_ref[...].astype(F32)).astype(BF16)


def ride_class(tile, rows, after):
    step = 4096
    last = pl.BlockSpec((step, PIECE), lambda i: (i, rows.shape[1] // PIECE - 1))
    return pl.pallas_call(
        ride_class_kernel,
        grid=(rows.shape[0] // step,),
        in_specs=[whole(tile), last, pl.BlockSpec(memory_space=pl.ANY)],
        out_specs=last,
        out_shape=jax.ShapeDtypeStruct(rows.shape, BF16),
        input_output_aliases={1: 0},
        compiler_params=params(MOST_MIB),
        name="ride_class",
    )(tile, rows, after)


def token(rows):
    return rows[:8, :128]


def exchange(rows):
    return lax.all_to_all(rows, BOTH, split_axis=0, concat_axis=0, tiled=True)


def on_device(
    features,
    hidden_weight,
    class_weight,
    req_owner,
    req_block,
    req_offset,
    hop1_counts,
    hop2_counts,
    prior_agg,
    prior_hop1,
    cotangent,
):
    outer, inner = lax.axis_size("gx"), lax.axis_size("gy")
    want, node = route(req_owner.reshape(1, -1), req_block, req_offset, hop2_counts)
    asked = lax.all_to_all(
        lax.all_to_all(
            want.reshape(outer, inner, LANES_CAP), "gx", split_axis=0, concat_axis=0, tiled=True
        ),
        "gy",
        split_axis=1,
        concat_axis=1,
        tiled=True,
    ).reshape(DEVICES, LANES_CAP)
    feat = features.shape[1]
    nodes = hop2_counts.shape[1]
    first = node[:, :FIRST].reshape(1, -1)
    tail = node[:, FIRST:CAP]
    folded = jnp.concatenate([tail, tail], axis=1).reshape(1, -1)
    last = node[:, CAP - 2 : CAP].reshape(1, -1)
    w2 = class_weight.T

    picked = gather(0, asked, features, asked)
    part0 = exchange(picked)
    core = (lax.axis_index("gx") % CORES).reshape(1)
    x = (lax.axis_index("gy") // Y).reshape(1)
    kept, sent = backward(
        core, prior_agg, prior_hop1, cotangent.T, hidden_weight, w2, token(picked)
    )
    own, *sent = split(x, kept, swap(sent, "gx", 1))
    got = [swap(rows, "gy", Y * k) for k, rows in enumerate(sent, 1)]
    picked = ride_sums(own, got, gather(1, asked, features, token(own)))
    part1 = exchange(picked)
    sums = sum_slots(first, part0, nodes)
    picked = gather(2, asked, features, token(picked))
    own, tile = own_sums(part1)
    part2 = exchange(ride_class(tile, picked, token(sums)))
    hidden_grad = own[: 2 * feat // PIECE].reshape(-1, 2, PIECE).transpose(1, 0, 2).reshape(2, -1).T
    pre, sums, *groups = sum_folded(
        folded, part1, sums, hop1_counts, hop2_counts, hidden_weight
    )
    logits, class_grad = forward(
        first, last, part2, sums, pre, *groups, hidden_weight, w2
    )
    logits, class_grad = logits.T, class_grad.T
    return (logits, hidden_grad, class_grad)


def solution(mesh):
    placed = (
        P(BOTH, None),
        P(),
        P(),
        P(BOTH, None, None),
        P(BOTH, None),
        P(BOTH, None),
        P(BOTH, None),
        P(BOTH, None),
        P(BOTH, None),
        P(BOTH, None),
        P(BOTH, None),
    )
    return jax.shard_map(
        on_device,
        mesh=mesh,
        in_specs=placed,
        out_specs=(P(BOTH, None), P(None, BOTH), P()),
        check_vma=False,
    )
```
